512 devices in a mesh: gx: 128 (over z, y, core), gy: 4 (over x).
Axes of the slice: x: 4, y: 8, z: 8, core: 2. Of those that a mesh axis runs over, the one named last changes fastest.
Arguments:
- source: float32 [64, 512, 8, 128], P(None, 'gx', 'gy'), may hold values from -6 to 6
- conductivity: float32 [512, 8, 128], P('gx', 'gy'), may hold values from 0.5 to 4
- diag_block: float32 [64, 64], replicated, as said below
- face_blocks: float32 [6, 64, 64], replicated
- smoother: float32 [64, 64], replicated
- prolong: float32 [4, 64, 64], replicated, may hold values from -0.75 to 0.75
Outputs:
- solution: float32 [64, 512, 8, 128], P(None, 'gx', 'gy')
- final_residual: float32 [64, 512, 8, 128], P(None, 'gx', 'gy')
The draws below stay inside these ranges and needn't reach their ends.
Inputs may be any that keep to these rules, and one draw needn't show every extreme that they name: diag_block has diagonal entries between 7 and 9 and small off-diagonal entries; face_blocks have diagonal entries between 0.7 and 1 and small off-diagonal entries; smoother has diagonal entries between 0.115 and 0.135 and small off-diagonal entries.
All inputs are finite; a program needn't handle non-finite values.
Results may differ from the reference program's by a relative error of at most 0.0003.
Values sent between devices are 32-bit elements; how exact they have to be, the bound alone decides.
A program may use at most 64 MiB of HBM per device.

```python
import math
import jax
import jax.numpy as jnp
from jax import lax

BLOCK = 64
COARSE_SWEEPS = 3
NX = 512
NY = 8
NZ = 128


def banded(key, shape, low, high, spread):
    key_diag, key_off = jax.random.split(key)
    identity = jnp.eye(BLOCK, dtype=jnp.float32)
    middle = jax.random.uniform(key_diag, shape, jnp.float32, low, high)
    offdiag = spread * jax.random.normal(key_off, shape, jnp.float32)
    return identity * middle + (1.0 - identity) * offdiag


def draw_diag_block(key, part):
    return banded(jax.random.fold_in(key, 11), (BLOCK, BLOCK), 7.0, 9.0, 0.04)


def draw_face_blocks(key, part):
    return banded(jax.random.fold_in(key, 12), (6, BLOCK, BLOCK), 0.7, 1.0, 0.015)


def draw_smoother(key, part):
    return banded(jax.random.fold_in(key, 13), (BLOCK, BLOCK), 0.115, 0.135, 0.002)


def block_scale(own_key, extent, cuts, low, largest):
    factor_of = 1.0
    for axis_at, blocks in cuts:
        heights = jax.random.uniform(jax.random.fold_in(jax.random.fold_in(own_key, 6), axis_at), (blocks,), jnp.float32, low / len(cuts), largest / len(cuts))
        factor_of = factor_of * jnp.repeat(jnp.exp(heights), extent[axis_at] // blocks).reshape((-1,) + (1,) * (len(extent) - 1 - axis_at))
    return factor_of


def noise(rng, extent, scale, reach, cuts=(), kind=jnp.bfloat16):
    entries = jax.random.normal(rng, extent, jnp.float32) * scale
    if len(cuts) > 0:
        entries = block_scale(rng, extent, cuts, -0.22, 0.18) * entries
    return jnp.clip(entries, min=-reach, max=reach).astype(kind)


def setup_inputs(seed: int = 0) -> dict:
    splits = jax.random.split(jax.random.key(seed), 7)
    source = noise(splits[0], (BLOCK, NX, NY, NZ), 1.0, 6.0, ((1, 128), (2, 4)), jnp.float32)
    conductivity = jnp.clip(jnp.exp(math.log(4.0) - 2.0794415 * jax.random.uniform(splits[1], (NX, NY, NZ), jnp.float32) ** block_scale(splits[1], (NX, NY, NZ), ((0, 128), (1, 4)), -0.2, 0.2)), 0.5, 4.0)
    diag_block = draw_diag_block(jax.random.fold_in(splits[6], 71), 0)
    face_blocks = draw_face_blocks(jax.random.fold_in(splits[6], 71), 0)
    smoother = draw_smoother(jax.random.fold_in(splits[6], 71), 0)
    prolong = noise(splits[5], (4, BLOCK, BLOCK), BLOCK ** -0.5, 0.75, (), jnp.float32)
    return {"source": source, "conductivity": conductivity, "diag_block": diag_block, "face_blocks": face_blocks, "smoother": smoother, "prolong": prolong}


OMEGA = 0.8


def multiply(matrix, values):
    return jnp.tensordot(matrix, values, axes=1, precision=lax.Precision.HIGHEST)


def neighbour(values, dim_id, offset):
    length = values.shape[dim_id]
    widths = [(0, 0)] * values.ndim
    widths[dim_id] = (1, 1)
    padded = jnp.pad(values, widths)
    return lax.slice_in_dim(padded, 1 + offset, 1 + offset + length, axis=dim_id)


def operate(values, coefficient, blocks):
    diag_block, face_blocks, smoother = blocks
    total_sum = multiply(diag_block, values)
    number = 0
    for dim_id in (1, 2, 3):
        for offset in (-1, 1):
            total_sum = total_sum - multiply(face_blocks[number], neighbour(values, dim_id, offset))
            number += 1
    return coefficient[None] * total_sum


def first_sweep(source, coefficient, blocks):
    return OMEGA * multiply(blocks[2], source / coefficient[None])


def sweep(iterate, source, coefficient, blocks):
    image = operate(iterate, coefficient, blocks)
    return iterate + OMEGA * multiply(blocks[2], (source - image) / coefficient[None])


def restrict_level(residual, coefficient, prolong):
    depth, span_x, span_y, span_z = residual.shape
    halves = residual.reshape(depth, span_x // 2, 2, span_y // 2, 2, span_z)
    tables = prolong.reshape(2, 2, depth, depth)
    coarse = 0.25 * jnp.einsum('acji,jxaycz->ixyz', tables, halves, precision=lax.Precision.HIGHEST)
    coarse_coef = jnp.mean(coefficient.reshape(span_x // 2, 2, span_y // 2, 2, span_z), axis=(1, 3))
    return coarse, coarse_coef


def prolong_level(coarse, prolong):
    depth, span_x, span_y, span_z = coarse.shape
    tables = prolong.reshape(2, 2, depth, depth)
    finer = jnp.einsum('acji,ixyz->jxaycz', tables, coarse, precision=lax.Precision.HIGHEST)
    return finer.reshape(depth, 2 * span_x, 2 * span_y, span_z)


def cycle(source, coefficient, blocks, prolong, level_id):
    iterate = first_sweep(source, coefficient, blocks)
    if level_id == 2:
        for sweep_id in range(COARSE_SWEEPS - 1):
            iterate = sweep(iterate, source, coefficient, blocks)
        return iterate
    iterate = sweep(iterate, source, coefficient, blocks)
    residual = source - operate(iterate, coefficient, blocks)
    coarse_source, coarse_coef = restrict_level(residual, coefficient, prolong)
    correction = cycle(coarse_source, coarse_coef, blocks, prolong, level_id + 1)
    iterate = iterate + prolong_level(correction, prolong)
    return sweep(iterate, source, coefficient, blocks)


def reference(source, conductivity, diag_block, face_blocks, smoother, prolong):
    blocks = (diag_block, face_blocks, smoother)
    solution = cycle(source, conductivity, blocks, prolong, 0)
    final_residual = source - operate(solution, conductivity, blocks)
    return solution, final_residual
```

```python
import functools

import jax
import jax.numpy as jnp
from jax import lax
from jax.experimental import pallas as pl
from jax.experimental.pallas import tpu as pltpu
from jax.sharding import PartitionSpec as P

MESH = pl.DeviceIdType.MESH
F32 = jnp.float32
BF16 = jnp.bfloat16
OMEGA = 0.8
N = 64
LANES = 128
XM, XP, YM, YP, CC, ZM, ZP, SM = (64 * i for i in range(8))
FACES = (XM, XP, YM, YP, ZM, ZP)


def split(v):
    hi = v.astype(BF16)
    lo = (v - hi.astype(F32)).astype(BF16)
    return jnp.concatenate([hi, lo, hi], axis=0)


def exact_dot(a, b):
    return jnp.dot(a, b, precision=lax.Precision.HIGHEST, preferred_element_type=F32)


def widen(w):
    hi = w.astype(BF16)
    lo = (w - hi.astype(F32)).astype(BF16)
    return jnp.concatenate([hi, hi, lo], axis=1)


def kernel(ngx, ngy, src, kap, diag, faces, smooth, prol, sol, res,
           q0, u1, u2, u3, q1, u11, u21, e1, q2, u12, u22, e2, pp, rr,
           wm, wl, wb, wr, wp,
           s_q0, r_q0, s_u2, r_u2, s_u2b, r_u2b, s_g, r_g, s_rl, r_rl, s_q2, r_q2, s_u21, r_u21):
    gx, gy = lax.axis_index("gx"), lax.axis_index("gy")

    def inside(dx, dy):
        ok = None
        for at, d, n in ((gx, dx, ngx), (gy, dy, ngy)):
            if d:
                c = (at + d >= 0) & (at + d < n)
                ok = c if ok is None else ok & c
        return ok

    barrier = pltpu.get_barrier_semaphore()
    partners = [(d, 0) for d in (-3, -2, -1, 1, 2, 3)] + [(0, d) for d in (-3, -2, -1, 1, 2, 3)]
    partners += [(a, b) for a in (-1, 1) for b in (-1, 1)]
    for dx, dy in partners:
        @pl.when(inside(dx, dy))
        def _():
            pl.semaphore_signal(barrier, inc=1, device_id=(gx + dx, gy + dy), device_id_type=MESH)
    for y in range(2):
        for x in range(4):
            c = x * 2 + y
            q0[1 + y, 1 + x] = src[pl.ds(c, N, stride=8), :] / kap[pl.ds(c, 1), :]
    peers = 0
    for dx, dy in partners:
        peers = peers + inside(dx, dy).astype(jnp.int32)
    pl.semaphore_wait(barrier, peers)

    def remote(s, d, ssem, rsem, dx, dy):
        return pltpu.make_async_remote_copy(
            src_ref=s, dst_ref=d, send_sem=ssem, recv_sem=rsem,
            device_id=(gx + dx, gy + dy), device_id_type=MESH)

    def send(s, d, ssem, rsem, dx, dy, cond=None):
        ok = inside(dx, dy) if cond is None else cond

        @pl.when(ok)
        def _():
            remote(s, d, ssem, rsem, dx, dy).start()

    def receive(d, ssem, rsem, dx, dy, cond=None):
        ok = inside(dx, dy) if cond is None else cond

        @pl.when(ok)
        def _():
            remote(d, d, ssem, rsem, dx, dy).wait_recv()

    def clear(ref, dx, dy):
        @pl.when(jnp.logical_not(inside(dx, dy)))
        def _():
            ref[...] = jnp.zeros(ref.shape, F32)

    def first_faces(buf, oy, ox):
        return [
            (buf.at[oy + 1, pl.ds(ox, 4)], buf.at[oy - 1, pl.ds(ox, 4)], 0, 1),
            (buf.at[oy, pl.ds(ox, 4)], buf.at[oy + 2, pl.ds(ox, 4)], 0, -1),
            (buf.at[pl.ds(oy, 2), ox + 3], buf.at[pl.ds(oy, 2), ox - 1], 1, 0),
            (buf.at[pl.ds(oy, 2), ox], buf.at[pl.ds(oy, 2), ox + 4], -1, 0),
        ]

    def second_faces(buf, oy, ox):
        return [
            (buf.at[oy, pl.ds(ox, 4)], buf.at[oy - 2, pl.ds(ox, 4)], 0, 1),
            (buf.at[oy + 1, pl.ds(ox, 4)], buf.at[oy + 3, pl.ds(ox, 4)], 0, -1),
            (buf.at[pl.ds(oy, 2), ox + 2], buf.at[pl.ds(oy, 2), ox - 2], 1, 0),
            (buf.at[pl.ds(oy, 2), ox + 1], buf.at[pl.ds(oy, 2), ox + 5], -1, 0),
            (buf.at[oy + 1, ox + 3], buf.at[oy - 1, ox - 1], 1, 1),
            (buf.at[oy + 1, ox], buf.at[oy - 1, ox + 4], -1, 1),
            (buf.at[oy, ox + 3], buf.at[oy + 2, ox - 1], 1, -1),
            (buf.at[oy, ox], buf.at[oy + 2, ox + 4], -1, -1),
        ]

    def send_all(faces_of, ssem, rsem):
        for i, (s, d, dx, dy) in enumerate(faces_of):
            send(s, d, ssem.at[i], rsem.at[i], dx, dy)

    def receive_all(faces_of, ssem, rsem):
        for i, (s, d, dx, dy) in enumerate(faces_of):
            receive(d, ssem.at[i], rsem.at[i], -dx, -dy)

    q0_faces = first_faces(q0, 1, 1)
    u2_faces = first_faces(u2, 2, 2)
    u2_more = second_faces(u2, 2, 2)
    send_all(q0_faces, s_q0, r_q0)

    s8 = OMEGA * smooth[...]
    eye = (lax.broadcasted_iota(jnp.int32, (N, N), 0) == lax.broadcasted_iota(jnp.int32, (N, N), 1)).astype(F32)
    wm[pl.ds(SM, N), :] = widen(s8)
    for i, at in enumerate(FACES):
        f = faces[i]
        wb[pl.ds(at, N), :] = widen(-f)
        sf = exact_dot(s8, f)
        wl[pl.ds(at, N), :] = widen(sf)
        wm[pl.ds(at, N), :] = widen(exact_dot(sf, s8))
    d = diag[...]
    wb[pl.ds(CC, N), :] = widen(d)
    lc = eye - exact_dot(s8, d)
    wl[pl.ds(CC, N), :] = widen(lc)
    wm[pl.ds(CC, N), :] = widen(s8 + exact_dot(lc, s8))
    for i in range(4):
        p = prol[i]
        wp[pl.ds(N * i, N), :] = widen(p)
        wr[pl.ds(N * i, N), :] = widen(0.25 * p.T)

    for buf, group in ((q0, q0_faces), (u2, u2_faces), (u2, u2_more)):
        for s, dst, dx, dy in group:
            clear(dst, -dx, -dy)
    clear(q1.at[pl.ds(0, 2)], -1, 0)
    clear(q1.at[pl.ds(4, 2)], 1, 0)
    clear(u21.at[0], -1, 0)
    clear(u21.at[5], 1, 0)
    for dd in (1, 2, 3):
        clear(q2.at[3 - dd], -dd, 0)
        clear(q2.at[3 + dd], dd, 0)
    e1[:, 0] = jnp.zeros((4, N, LANES), F32)
    e1[:, 5] = jnp.zeros((4, N, LANES), F32)

    lane = lax.broadcasted_iota(jnp.int32, (N, LANES), 1)
    not_first, not_last = lane > 0, lane < LANES - 1

    def apply(w, row, rows, load, cols, at):
        pair = jnp.concatenate([split(load(cols[0])), split(load(cols[1]))], axis=1)
        out = jnp.dot(w[pl.ds(row, rows), :], pair, preferred_element_type=F32)
        pp[at[0], pl.ds(row, rows), :] = out[:, :LANES]
        pp[at[1], pl.ds(row, rows), :] = out[:, LANES:]

    def gathered(c, sx, sy, ym=True, yp=True):
        t = pp[c, pl.ds(CC, N), :]
        t = t + pp[c - sx, pl.ds(XM, N), :] + pp[c + sx, pl.ds(XP, N), :]
        if ym:
            t = t + pp[c - sy, pl.ds(YM, N), :]
        if yp:
            t = t + pp[c + sy, pl.ds(YP, N), :]
        t = t + jnp.where(not_first, pltpu.roll(pp[c, pl.ds(ZM, N), :], 1, 1), 0.0)
        t = t + jnp.where(not_last, pltpu.roll(pp[c, pl.ds(ZP, N), :], LANES - 1, 1), 0.0)
        return t

    def loop(n, body):
        def step(i, carry):
            body(i)
            return carry
        lax.fori_loop(0, n, step, 0)

    def fine_at(y, x):
        return (y + 2) * 8 + x + 2

    def fine_own(w, rows, buf, oy, ox):
        def body(i):
            y, x = i // 2, (i % 2) * 2
            apply(w, 0, rows, lambda c: buf[oy + c[0], ox + c[1]], ((y, x), (y, x + 1)),
                  (fine_at(y, x), fine_at(y, x + 1)))
        loop(4, body)

    def fine_edges(w, buf, oy, ox):
        def load(c):
            return buf[oy + c[0], ox + c[1]]

        def body_x(y):
            apply(w, XM, 128, load, ((y, -1), (y, 4)), (fine_at(y, -1), fine_at(y, 4)))
        loop(2, body_x)

        def body_y(x):
            apply(w, YM, 128, load, ((-1, x), (2, x)), (fine_at(-1, x), fine_at(2, x)))
        loop(4, body_y)

    fine_own(wm, 512, q0, 1, 1)
    receive_all(q0_faces, s_q0, r_q0)
    fine_edges(wm, q0, 1, 1)

    def sum_u2(i):
        y, x = i // 4, i % 4
        c = fine_at(y, x)
        u2[2 + y, 2 + x] = gathered(c, 1, 8)
        u1[1 + y, 1 + x] = pp[c, pl.ds(SM, N), :]
    loop(8, sum_u2)
    send_all(u2_faces, s_u2, r_u2)

    fine_own(wb, 448, u2, 2, 2)

    def ring_u1(y, x, y2, x2):
        pair = jnp.concatenate([split(q0[1 + y, 1 + x]), split(q0[1 + y2, 1 + x2])], axis=1)
        out = jnp.dot(wm[pl.ds(SM, N), :], pair, preferred_element_type=F32)
        u1[1 + y, 1 + x] = out[:, :LANES]
        u1[1 + y2, 1 + x2] = out[:, LANES:]
    loop(2, lambda y: ring_u1(y, -1, y, 4))
    loop(4, lambda x: ring_u1(-1, x, 2, x))
    receive_all(u2_faces, s_u2, r_u2)
    fine_edges(wb, u2, 2, 2)

    def sum_r0(i):
        y, x = i // 4, i % 4
        t = gathered(fine_at(y, x), 1, 8)
        k = kap[pl.ds(x * 2 + y, 1), :]
        rr[i] = split((q0[1 + y, 1 + x] - t) * k)
    loop(8, sum_r0)

    def restrict(index):
        total = None
        for child in range(4):
            pair = jnp.concatenate([rr[index(0, child)], rr[index(1, child)]], axis=1)
            part = jnp.dot(wr[pl.ds(N * child, N), :], pair, preferred_element_type=F32)
            total = part if total is None else total + part
        return total[:, :LANES], total[:, LANES:]

    coarse = restrict(lambda at, child: (child % 2) * 4 + 2 * at + child // 2)
    for at in range(2):
        k1 = kap[pl.ds(4 * at, 1), :] + kap[pl.ds(4 * at + 1, 1), :]
        k1 = (k1 + (kap[pl.ds(4 * at + 2, 1), :] + kap[pl.ds(4 * at + 3, 1), :])) * 0.25
        q1[2 + at, gy, pl.ds(0, N), :] = coarse[at] / k1
        q1[2 + at, gy, pl.ds(N, 8), :] = jnp.broadcast_to(k1, (8, LANES))

    for j in range(ngy):
        own = q1.at[pl.ds(2, 2), gy]
        cond = gy != j

        @pl.when(cond)
        def _():
            pltpu.make_async_remote_copy(
                src_ref=own, dst_ref=own, send_sem=s_g.at[j], recv_sem=r_g.at[gy],
                device_id=(gx, j), device_id_type=MESH).start()

    def relay(j):
        block = q1.at[pl.ds(2, 2), j]
        for i, (dx, at) in enumerate(((1, 0), (-1, 4))):
            @pl.when(inside(dx, 0))
            def _():
                remote(block, q1.at[pl.ds(at, 2), j], s_rl.at[i, j], r_rl.at[i, j], dx, 0).start()

    relay(gy)
    send_all(u2_more, s_u2b, r_u2b)

    def arrive(j):
        block = q1.at[pl.ds(2, 2), j]
        pltpu.make_async_remote_copy(
            src_ref=block, dst_ref=block, send_sem=s_g.at[j], recv_sem=r_g.at[j],
            device_id=(gx, j), device_id_type=MESH).wait_recv()
        relay(j)
    for dd in (1, -1, 2, -2, 3, -3):
        @pl.when(inside(0, dd))
        def _():
            arrive(gy + dd)

    def coarse_own(w, rows, load, first, planes):
        def body(i):
            c = 4 * first + 2 * i
            apply(w, 0, rows, load, (c, c + 1), (c, c + 1))
        loop(2 * planes, body)

    def coarse_edges(w, load, low, high):
        def body(y):
            c, e = 4 * low + y, 4 * high + y
            apply(w, XM, 128, load, (c, e), (c, e))
        loop(4, body)

    def load_q1(c):
        return q1[c // 4, c % 4, pl.ds(0, N), :]

    def load_u21(c):
        return u21[c // 4, c % 4]

    coarse_own(wm, 512, load_q1, 2, 2)
    for j in range(ngy):
        for i, (dx, at) in enumerate(((1, 0), (-1, 4))):
            @pl.when(inside(-dx, 0))
            def _():
                block = q1.at[pl.ds(at, 2), j]
                remote(block, block, s_rl.at[i, j], r_rl.at[i, j], -dx, 0).wait_recv()
    coarse_own(wm, 512, load_q1, 1, 1)
    coarse_own(wm, 512, load_q1, 4, 1)
    coarse_edges(wm, load_q1, 0, 5)

    def keep(ok):
        return jnp.where(ok, 1.0, 0.0).astype(F32)

    def present(offset):
        return keep((gx + offset >= 0) & (gx + offset < ngx))

    def device_of(x):
        return (x // 2) - 1

    def sum_u21(x):
        m = present(device_of(x))
        for y in range(4):
            c = 4 * x + y
            u21[x, y] = m * gathered(c, 4, 1, y > 0, y < 3)
            u11[x, y] = m * pp[c, pl.ds(SM, N), :]
    loop(4, lambda i: sum_u21(i + 1))

    coarse_own(wb, 448, load_u21, 2, 2)
    coarse_edges(wb, load_u21, 1, 4)

    def sum_r1(x):
        for y in range(4):
            t = gathered(4 * x + y, 4, 1, y > 0, y < 3)
            k1 = q1[x, y, pl.ds(N, 1), :]
            rr[(x - 2) * 4 + y] = split((q1[x, y, pl.ds(0, N), :] - t) * k1)
    loop(2, lambda i: sum_r1(i + 2))
    coarse2 = restrict(lambda at, child: (child // 2) * 4 + 2 * at + child % 2)
    for at in range(2):
        k2 = q1[2, 2 * at, pl.ds(N, 1), :] + q1[2, 2 * at + 1, pl.ds(N, 1), :]
        k2 = (k2 + (q1[3, 2 * at, pl.ds(N, 1), :] + q1[3, 2 * at + 1, pl.ds(N, 1), :])) * 0.25
        q2[3, at] = coarse2[at] / k2

    q2_moves = [(q2.at[3], q2.at[3 - dd], dd, 0) for dd in (1, -1, 2, -2, 3, -3)]
    send_all(q2_moves, s_q2, r_q2)
    u21_moves = [(u21.at[2], u21.at[0], 1, 0), (u21.at[3], u21.at[5], -1, 0)]
    send_all(u21_moves, s_u21, r_u21)

    def load_q2(c):
        return q2[c // 2, c % 2]

    def load_u22(c):
        return u22[c // 2, c % 2]

    def last_own(w, rows, load, first, planes):
        def body(i):
            c = 2 * first + 2 * i
            apply(w, 0, rows, load, (c, c + 1), (c, c + 1))
        loop(planes, body)

    def last_edges(w, load, low, high):
        def body(y):
            c, e = 2 * low + y, 2 * high + y
            apply(w, XM, 128, load, (c, e), (c, e))
        loop(2, body)

    last_own(wm, 512, load_q2, 3, 1)
    receive_all(q2_moves, s_q2, r_q2)
    last_own(wm, 512, load_q2, 1, 2)
    last_own(wm, 512, load_q2, 4, 2)
    last_edges(wm, load_q2, 0, 6)

    def sum_u22(x):
        m = present(x - 3)
        for y in range(2):
            u22[x, y] = m * gathered(2 * x + y, 2, 1, y > 0, y < 1)
            u12[x, y] = pp[2 * x + y, pl.ds(SM, N), :]
    loop(5, lambda i: sum_u22(i + 1))
    last_own(wl, 448, load_u22, 2, 3)
    last_edges(wl, load_u22, 1, 5)

    def sum_e2(x):
        m = present(x - 3)
        for y in range(2):
            e2[x - 2, y] = m * (u12[x, y] + gathered(2 * x + y, 2, 1, y > 0, y < 1))
    loop(3, lambda i: sum_e2(i + 2))

    receive_all(u21_moves, s_u21, r_u21)

    def prolong(load):
        pair = jnp.concatenate([split(load(0)), split(load(1))], axis=1)
        out = jnp.dot(wp[...], pair, preferred_element_type=F32)
        return lambda at, child: out[N * child:N * (child + 1), LANES * at:LANES * (at + 1)]

    for i, (s, dst, dx, dy) in enumerate(u21_moves):
        @pl.when(inside(dx, dy))
        def _():
            remote(s, dst, s_u21.at[i], r_u21.at[i], dx, dy).wait_send()

    def lift1(x2):
        part = prolong(lambda y: e2[x2, y])
        for y2 in range(2):
            for child in range(4):
                x, y = 2 * x2 + child // 2, 2 * y2 + child % 2
                u21[x, y] = u21[x, y] + part(y2, child)
    loop(3, lift1)
    coarse_own(wl, 448, load_u21, 1, 4)
    coarse_edges(wl, load_u21, 0, 5)

    def sum_e1(x):
        m = present(device_of(x))
        for y in range(4):
            e1[x - 1, 1 + y] = m * (u11[x, y] + gathered(4 * x + y, 4, 1, y > 0, y < 3))
    loop(4, lambda i: sum_e1(i + 1))

    for i, (s, dst, dx, dy) in enumerate(u2_faces):
        @pl.when(inside(dx, dy))
        def _():
            remote(s, dst, s_u2.at[i], r_u2.at[i], dx, dy).wait_send()
    receive_all(u2_more, s_u2b, r_u2b)
    for i, (s, dst, dx, dy) in enumerate(u2_more):
        @pl.when(inside(dx, dy))
        def _():
            remote(s, dst, s_u2b.at[i], r_u2b.at[i], dx, dy).wait_send()

    wanted = {(y, x) for y in range(-2, 4) for x in range(-2, 6)
              if max(0, -y, y - 1) + max(0, -x, x - 3) <= 2}
    for j in range(3):
        for xp in range(2):
            part = prolong(lambda i: e1[2 * xp + i, gy + j])
            for i in range(2):
                for child in range(4):
                    x = 2 * (2 * xp + i - 1) + child // 2
                    y = 2 * (j - 1) + child % 2
                    if (y, x) in wanted:
                        u2[2 + y, 2 + x] = u2[2 + y, 2 + x] + part(i, child)

    def load_u2(c):
        return u2[2 + c[0], 2 + c[1]]

    def both(w, row, rows, c, e):
        apply(w, row, rows, load_u2, (c, e), (fine_at(*c), fine_at(*e)))

    def rows_wide(i):
        y, x = i // 3, (i % 3) * 2 - 1
        both(wl, 0, 448, (y, x), (y, x + 1))
    loop(6, rows_wide)

    def rows_short(i):
        y, x = (i // 2) * 3 - 1, (i % 2) * 2
        both(wl, 0, 448, (y, x), (y, x + 1))
    loop(4, rows_short)
    loop(2, lambda y: both(wl, XM, 128, (y, -2), (y, 5)))
    loop(4, lambda x: both(wl, YM, 128, (-2, x), (3, x)))
    loop(2, lambda i: both(wl, 0, 256, (3 * i - 1, -1), (3 * i - 1, 4)))

    def sum_u3(y, x, m=None):
        v = u1[1 + y, 1 + x] + gathered(fine_at(y, x), 1, 8)
        u3[1 + y, 1 + x] = v if m is None else m * v
        return v

    def own_u3(i):
        y, x = i // 4, i % 4
        v = sum_u3(y, x)
        sol[pl.ds(x * 2 + y, N, stride=8), :] = v
    loop(8, own_u3)
    loop(2, lambda y: sum_u3(y, -1, present(-1)))
    loop(2, lambda y: sum_u3(y, 4, present(1)))
    loop(4, lambda x: sum_u3(-1, x, keep(gy > 0)))
    loop(4, lambda x: sum_u3(2, x, keep(gy < ngy - 1)))
    fine_own(wb, 448, u3, 1, 1)
    fine_edges(wb, u3, 1, 1)

    def final(i):
        y, x = i // 4, i % 4
        c = x * 2 + y
        t = gathered(fine_at(y, x), 1, 8)
        res[pl.ds(c, N, stride=8), :] = src[pl.ds(c, N, stride=8), :] - kap[pl.ds(c, 1), :] * t
    loop(8, final)

    for group, ssem, rsem in ((q0_faces, s_q0, r_q0), (q2_moves, s_q2, r_q2)):
        for i, (s, dst, dx, dy) in enumerate(group):
            @pl.when(inside(dx, dy))
            def _():
                remote(s, dst, ssem.at[i], rsem.at[i], dx, dy).wait_send()
    for j in range(ngy):
        block = q1.at[pl.ds(2, 2), j]

        @pl.when(gy != j)
        def _():
            pltpu.make_async_remote_copy(
                src_ref=block, dst_ref=block, send_sem=s_g.at[j], recv_sem=r_g.at[j],
                device_id=(gx, j), device_id_type=MESH).wait_send()
        for i, (dx, at) in enumerate(((1, 0), (-1, 4))):
            @pl.when(inside(dx, 0))
            def _():
                remote(block, q1.at[pl.ds(at, 2), j], s_rl.at[i, j], r_rl.at[i, j], dx, 0).wait_send()


def solution(mesh):
    ngx, ngy = mesh.shape["gx"], mesh.shape["gy"]

    def shards(source, conductivity, diag_block, face_blocks, smoother, prolong):
        dma = pltpu.SemaphoreType.DMA
        col = (N, LANES)
        scratch = [
            pltpu.VMEM((4, 6) + col, F32),
            pltpu.VMEM((4, 6) + col, F32),
            pltpu.VMEM((6, 8) + col, F32),
            pltpu.VMEM((4, 6) + col, F32),
            pltpu.VMEM((6, 4, N + 8, LANES), F32),
            pltpu.VMEM((6, 4) + col, F32),
            pltpu.VMEM((6, 4) + col, F32),
            pltpu.VMEM((4, 6) + col, F32),
            pltpu.VMEM((7, 2) + col, F32),
            pltpu.VMEM((7, 2) + col, F32),
            pltpu.VMEM((7, 2) + col, F32),
            pltpu.VMEM((3, 2) + col, F32),
            pltpu.VMEM((48, 512, LANES), F32),
            pltpu.VMEM((8, 192, LANES), BF16),
            pltpu.VMEM((512, 192), BF16),
            pltpu.VMEM((448, 192), BF16),
            pltpu.VMEM((448, 192), BF16),
            pltpu.VMEM((256, 192), BF16),
            pltpu.VMEM((256, 192), BF16),
            dma((4,)), dma((4,)), dma((4,)), dma((4,)), dma((8,)), dma((8,)),
            dma((4,)), dma((4,)), dma((2, 4)), dma((2, 4)), dma((6,)), dma((6,)), dma((2,)), dma((2,)),
        ]
        shape = source.shape
        flat = jax.ShapeDtypeStruct((N * 8, LANES), F32)
        vmem = pl.BlockSpec(memory_space=pltpu.VMEM)
        sol, res = pl.pallas_call(
            functools.partial(kernel, ngx, ngy),
            out_shape=(flat, flat),
            in_specs=[vmem] * 6,
            out_specs=(vmem, vmem),
            scratch_shapes=scratch,
            compiler_params=pltpu.CompilerParams(
                collective_id=0, has_side_effects=True, vmem_limit_bytes=40 << 20),
            cost_estimate=pl.CostEstimate(flops=10**9, bytes_accessed=10**6, transcendentals=0),
        )(source.reshape(N * 8, LANES), conductivity.reshape(8, LANES),
          diag_block, face_blocks, smoother, prolong)
        return sol.reshape(shape), res.reshape(shape)

    return jax.shard_map(
        shards,
        mesh=mesh,
        in_specs=(P(None, "gx", "gy", None), P("gx", "gy", None), P(), P(), P(), P()),
        out_specs=(P(None, "gx", "gy", None), P(None, "gx", "gy", None)),
        check_vma=False,
    )
```

```python
import functools

import jax
import jax.numpy as jnp
from jax import lax
from jax.experimental import pallas as pl
from jax.experimental.pallas import tpu as pltpu
from jax.sharding import PartitionSpec as P

MESH = pl.DeviceIdType.MESH
F32 = jnp.float32
BF16 = jnp.bfloat16
OMEGA = 0.8
N = 64
LANES = 128
XM, XP, YM, YP, CC, ZM, ZP, SM = (64 * i for i in range(8))
FACES = (XM, XP, YM, YP, ZM, ZP)


def split(v):
    hi = v.astype(BF16)
    lo = (v - hi.astype(F32)).astype(BF16)
    return jnp.concatenate([hi, lo, hi], axis=0)


def exact_dot(a, b):
    return jnp.dot(a, b, precision=lax.Precision.HIGHEST, preferred_element_type=F32)


def widen(w):
    hi = w.astype(BF16)
    lo = (w - hi.astype(F32)).astype(BF16)
    return jnp.concatenate([hi, hi, lo], axis=1)


def kernel(ngx, ngy, src, kap, diag, faces, smooth, prol, sol, res,
           q0, u1, u2, u3, q1, u11, u21, e1, q2, u12, u22, e2, pp, rr,
           wm, wl, wb, wr, wp,
           s_q0, r_q0, s_u2, r_u2, s_u2b, r_u2b, s_g, r_g, s_rl, r_rl, s_q2, r_q2, s_u21, r_u21):
    gx, gy = lax.axis_index("gx"), lax.axis_index("gy")

    def inside(dx, dy):
        ok = None
        for at, d, n in ((gx, dx, ngx), (gy, dy, ngy)):
            if d:
                c = (at + d >= 0) & (at + d < n)
                ok = c if ok is None else ok & c
        return ok

    barrier = pltpu.get_barrier_semaphore()
    partners = [(d, 0) for d in (-3, -2, -1, 1, 2, 3)] + [(0, d) for d in (-3, -2, -1, 1, 2, 3)]
    partners += [(a, b) for a in (-1, 1) for b in (-1, 1)]
    for dx, dy in partners:
        @pl.when(inside(dx, dy))
        def _():
            pl.semaphore_signal(barrier, inc=1, device_id=(gx + dx, gy + dy), device_id_type=MESH)
    for y in range(2):
        for x in range(4):
            c = x * 2 + y
            q0[1 + y, 1 + x] = src[pl.ds(c, N, stride=8), :] / kap[pl.ds(c, 1), :]
    peers = 0
    for dx, dy in partners:
        peers = peers + inside(dx, dy).astype(jnp.int32)
    pl.semaphore_wait(barrier, peers)

    def remote(s, d, ssem, rsem, dx, dy):
        return pltpu.make_async_remote_copy(
            src_ref=s, dst_ref=d, send_sem=ssem, recv_sem=rsem,
            device_id=(gx + dx, gy + dy), device_id_type=MESH)

    def send(s, d, ssem, rsem, dx, dy, cond=None):
        ok = inside(dx, dy) if cond is None else cond

        @pl.when(ok)
        def _():
            remote(s, d, ssem, rsem, dx, dy).start()

    def receive(d, ssem, rsem, dx, dy, cond=None):
        ok = inside(dx, dy) if cond is None else cond

        @pl.when(ok)
        def _():
            remote(d, d, ssem, rsem, dx, dy).wait_recv()

    def clear(ref, dx, dy):
        @pl.when(jnp.logical_not(inside(dx, dy)))
        def _():
            ref[...] = jnp.zeros(ref.shape, F32)

    def first_faces(buf, oy, ox):
        return [
            (buf.at[oy + 1, pl.ds(ox, 4)], buf.at[oy - 1, pl.ds(ox, 4)], 0, 1),
            (buf.at[oy, pl.ds(ox, 4)], buf.at[oy + 2, pl.ds(ox, 4)], 0, -1),
            (buf.at[pl.ds(oy, 2), ox + 3], buf.at[pl.ds(oy, 2), ox - 1], 1, 0),
            (buf.at[pl.ds(oy, 2), ox], buf.at[pl.ds(oy, 2), ox + 4], -1, 0),
        ]

    def second_faces(buf, oy, ox):
        return [
            (buf.at[oy, pl.ds(ox, 4)], buf.at[oy - 2, pl.ds(ox, 4)], 0, 1),
            (buf.at[oy + 1, pl.ds(ox, 4)], buf.at[oy + 3, pl.ds(ox, 4)], 0, -1),
            (buf.at[pl.ds(oy, 2), ox + 2], buf.at[pl.ds(oy, 2), ox - 2], 1, 0),
            (buf.at[pl.ds(oy, 2), ox + 1], buf.at[pl.ds(oy, 2), ox + 5], -1, 0),
            (buf.at[oy + 1, ox + 3], buf.at[oy - 1, ox - 1], 1, 1),
            (buf.at[oy + 1, ox], buf.at[oy - 1, ox + 4], -1, 1),
            (buf.at[oy, ox + 3], buf.at[oy + 2, ox - 1], 1, -1),
            (buf.at[oy, ox], buf.at[oy + 2, ox + 4], -1, -1),
        ]

    def send_all(faces_of, ssem, rsem):
        for i, (s, d, dx, dy) in enumerate(faces_of):
            send(s, d, ssem.at[i], rsem.at[i], dx, dy)

    def receive_all(faces_of, ssem, rsem):
        for i, (s, d, dx, dy) in enumerate(faces_of):
            receive(d, ssem.at[i], rsem.at[i], -dx, -dy)

    q0_faces = first_faces(q0, 1, 1)
    u2_faces = first_faces(u2, 2, 2)
    u2_more = second_faces(u2, 2, 2)
    send_all(q0_faces, s_q0, r_q0)

    s8 = OMEGA * smooth[...]
    eye = (lax.broadcasted_iota(jnp.int32, (N, N), 0) == lax.broadcasted_iota(jnp.int32, (N, N), 1)).astype(F32)
    wm[pl.ds(SM, N), :] = widen(s8)
    for i, at in enumerate(FACES):
        f = faces[i]
        wb[pl.ds(at, N), :] = widen(-f)
        sf = exact_dot(s8, f)
        wl[pl.ds(at, N), :] = widen(sf)
        wm[pl.ds(at, N), :] = widen(exact_dot(sf, s8))
    d = diag[...]
    wb[pl.ds(CC, N), :] = widen(d)
    lc = eye - exact_dot(s8, d)
    wl[pl.ds(CC, N), :] = widen(lc)
    wm[pl.ds(CC, N), :] = widen(s8 + exact_dot(lc, s8))
    for i in range(4):
        p = prol[i]
        wp[pl.ds(N * i, N), :] = widen(p)
        wr[pl.ds(N * i, N), :] = widen(0.25 * p.T)

    for buf, group in ((q0, q0_faces), (u2, u2_faces), (u2, u2_more)):
        for s, dst, dx, dy in group:
            clear(dst, -dx, -dy)
    clear(q1.at[pl.ds(0, 2)], -1, 0)
    clear(q1.at[pl.ds(4, 2)], 1, 0)
    clear(u21.at[0], -1, 0)
    clear(u21.at[5], 1, 0)
    for dd in (1, 2, 3):
        clear(q2.at[3 - dd], -dd, 0)
        clear(q2.at[3 + dd], dd, 0)
    e1[:, 0] = jnp.zeros((4, N, LANES), F32)
    e1[:, 5] = jnp.zeros((4, N, LANES), F32)

    lane = lax.broadcasted_iota(jnp.int32, (N, LANES), 1)
    not_first, not_last = lane > 0, lane < LANES - 1

    def apply(w, row, rows, load, cols, at):
        pair = jnp.concatenate([split(load(cols[0])), split(load(cols[1]))], axis=1)
        out = jnp.dot(w[pl.ds(row, rows), :], pair, preferred_element_type=F32)
        pp[at[0], pl.ds(row, rows), :] = out[:, :LANES]
        pp[at[1], pl.ds(row, rows), :] = out[:, LANES:]

    def gathered(c, sx, sy, ym=True, yp=True):
        t = pp[c, pl.ds(CC, N), :]
        t = t + pp[c - sx, pl.ds(XM, N), :] + pp[c + sx, pl.ds(XP, N), :]
        if ym:
            t = t + pp[c - sy, pl.ds(YM, N), :]
        if yp:
            t = t + pp[c + sy, pl.ds(YP, N), :]
        t = t + jnp.where(not_first, pltpu.roll(pp[c, pl.ds(ZM, N), :], 1, 1), 0.0)
        t = t + jnp.where(not_last, pltpu.roll(pp[c, pl.ds(ZP, N), :], LANES - 1, 1), 0.0)
        return t

    def loop(n, body):
        for i in range(n):
            body(i)

    def fine_at(y, x):
        return (y + 2) * 8 + x + 2

    def fine_own(w, rows, buf, oy, ox):
        def body(i):
            y, x = i // 2, (i % 2) * 2
            apply(w, 0, rows, lambda c: buf[oy + c[0], ox + c[1]], ((y, x), (y, x + 1)),
                  (fine_at(y, x), fine_at(y, x + 1)))
        loop(4, body)

    def fine_edges(w, buf, oy, ox):
        def load(c):
            return buf[oy + c[0], ox + c[1]]

        def body_x(y):
            apply(w, XM, 128, load, ((y, -1), (y, 4)), (fine_at(y, -1), fine_at(y, 4)))
        loop(2, body_x)

        def body_y(x):
            apply(w, YM, 128, load, ((-1, x), (2, x)), (fine_at(-1, x), fine_at(2, x)))
        loop(4, body_y)

    fine_own(wm, 512, q0, 1, 1)
    receive_all(q0_faces, s_q0, r_q0)
    fine_edges(wm, q0, 1, 1)

    def sum_u2(i):
        y, x = i // 4, i % 4
        c = fine_at(y, x)
        u2[2 + y, 2 + x] = gathered(c, 1, 8)
        u1[1 + y, 1 + x] = pp[c, pl.ds(SM, N), :]
    loop(8, sum_u2)
    send_all(u2_faces, s_u2, r_u2)

    fine_own(wb, 448, u2, 2, 2)

    def ring_u1(y, x, y2, x2):
        pair = jnp.concatenate([split(q0[1 + y, 1 + x]), split(q0[1 + y2, 1 + x2])], axis=1)
        out = jnp.dot(wm[pl.ds(SM, N), :], pair, preferred_element_type=F32)
        u1[1 + y, 1 + x] = out[:, :LANES]
        u1[1 + y2, 1 + x2] = out[:, LANES:]
    loop(2, lambda y: ring_u1(y, -1, y, 4))
    loop(4, lambda x: ring_u1(-1, x, 2, x))
    receive_all(u2_faces, s_u2, r_u2)
    fine_edges(wb, u2, 2, 2)

    def sum_r0(i):
        y, x = i // 4, i % 4
        t = gathered(fine_at(y, x), 1, 8)
        k = kap[pl.ds(x * 2 + y, 1), :]
        rr[i] = split((q0[1 + y, 1 + x] - t) * k)
    loop(8, sum_r0)

    def restrict(index):
        total = None
        for child in range(4):
            pair = jnp.concatenate([rr[index(0, child)], rr[index(1, child)]], axis=1)
            part = jnp.dot(wr[pl.ds(N * child, N), :], pair, preferred_element_type=F32)
            total = part if total is None else total + part
        return total[:, :LANES], total[:, LANES:]

    coarse = restrict(lambda at, child: (child % 2) * 4 + 2 * at + child // 2)
    for at in range(2):
        k1 = kap[pl.ds(4 * at, 1), :] + kap[pl.ds(4 * at + 1, 1), :]
        k1 = (k1 + (kap[pl.ds(4 * at + 2, 1), :] + kap[pl.ds(4 * at + 3, 1), :])) * 0.25
        q1[2 + at, gy, pl.ds(0, N), :] = coarse[at] / k1
        q1[2 + at, gy, pl.ds(N, 8), :] = jnp.broadcast_to(k1, (8, LANES))

    for j in range(ngy):
        own = q1.at[pl.ds(2, 2), gy]
        cond = gy != j

        @pl.when(cond)
        def _():
            pltpu.make_async_remote_copy(
                src_ref=own, dst_ref=own, send_sem=s_g.at[j], recv_sem=r_g.at[gy],
                device_id=(gx, j), device_id_type=MESH).start()

    def relay(j):
        block = q1.at[pl.ds(2, 2), j]
        for i, (dx, at) in enumerate(((1, 0), (-1, 4))):
            @pl.when(inside(dx, 0))
            def _():
                remote(block, q1.at[pl.ds(at, 2), j], s_rl.at[i, j], r_rl.at[i, j], dx, 0).start()

    relay(gy)
    send_all(u2_more, s_u2b, r_u2b)

    def arrive(j):
        block = q1.at[pl.ds(2, 2), j]
        pltpu.make_async_remote_copy(
            src_ref=block, dst_ref=block, send_sem=s_g.at[j], recv_sem=r_g.at[j],
            device_id=(gx, j), device_id_type=MESH).wait_recv()
        relay(j)
    for dd in (1, -1, 2, -2, 3, -3):
        @pl.when(inside(0, dd))
        def _():
            arrive(gy + dd)

    def coarse_own(w, rows, load, first, planes):
        def body(i):
            c = 4 * first + 2 * i
            apply(w, 0, rows, load, (c, c + 1), (c, c + 1))
        loop(2 * planes, body)

    def coarse_edges(w, load, low, high):
        def body(y):
            c, e = 4 * low + y, 4 * high + y
            apply(w, XM, 128, load, (c, e), (c, e))
        loop(4, body)

    def load_q1(c):
        return q1[c // 4, c % 4, pl.ds(0, N), :]

    def load_u21(c):
        return u21[c // 4, c % 4]

    coarse_own(wm, 512, load_q1, 2, 2)
    for j in range(ngy):
        for i, (dx, at) in enumerate(((1, 0), (-1, 4))):
            @pl.when(inside(-dx, 0))
            def _():
                block = q1.at[pl.ds(at, 2), j]
                remote(block, block, s_rl.at[i, j], r_rl.at[i, j], -dx, 0).wait_recv()
    coarse_own(wm, 512, load_q1, 1, 1)
    coarse_own(wm, 512, load_q1, 4, 1)
    coarse_edges(wm, load_q1, 0, 5)

    def keep(ok):
        return jnp.where(ok, 1.0, 0.0).astype(F32)

    def present(offset):
        return keep((gx + offset >= 0) & (gx + offset < ngx))

    def device_of(x):
        return (x // 2) - 1

    def sum_u21(x):
        m = present(device_of(x))
        for y in range(4):
            c = 4 * x + y
            u21[x, y] = m * gathered(c, 4, 1, y > 0, y < 3)
            u11[x, y] = m * pp[c, pl.ds(SM, N), :]
    loop(4, lambda i: sum_u21(i + 1))

    coarse_own(wb, 448, load_u21, 2, 2)
    coarse_edges(wb, load_u21, 1, 4)

    def sum_r1(x):
        for y in range(4):
            t = gathered(4 * x + y, 4, 1, y > 0, y < 3)
            k1 = q1[x, y, pl.ds(N, 1), :]
            rr[(x - 2) * 4 + y] = split((q1[x, y, pl.ds(0, N), :] - t) * k1)
    loop(2, lambda i: sum_r1(i + 2))
    coarse2 = restrict(lambda at, child: (child // 2) * 4 + 2 * at + child % 2)
    for at in range(2):
        k2 = q1[2, 2 * at, pl.ds(N, 1), :] + q1[2, 2 * at + 1, pl.ds(N, 1), :]
        k2 = (k2 + (q1[3, 2 * at, pl.ds(N, 1), :] + q1[3, 2 * at + 1, pl.ds(N, 1), :])) * 0.25
        q2[3, at] = coarse2[at] / k2

    q2_moves = [(q2.at[3], q2.at[3 - dd], dd, 0) for dd in (1, -1, 2, -2, 3, -3)]
    send_all(q2_moves, s_q2, r_q2)
    u21_moves = [(u21.at[2], u21.at[0], 1, 0), (u21.at[3], u21.at[5], -1, 0)]
    send_all(u21_moves, s_u21, r_u21)

    def load_q2(c):
        return q2[c // 2, c % 2]

    def load_u22(c):
        return u22[c // 2, c % 2]

    def last_own(w, rows, load, first, planes):
        def body(i):
            c = 2 * first + 2 * i
            apply(w, 0, rows, load, (c, c + 1), (c, c + 1))
        loop(planes, body)

    def last_edges(w, load, low, high):
        def body(y):
            c, e = 2 * low + y, 2 * high + y
            apply(w, XM, 128, load, (c, e), (c, e))
        loop(2, body)

    last_own(wm, 512, load_q2, 3, 1)
    receive_all(q2_moves, s_q2, r_q2)
    last_own(wm, 512, load_q2, 1, 2)
    last_own(wm, 512, load_q2, 4, 2)
    last_edges(wm, load_q2, 0, 6)

    def sum_u22(x):
        m = present(x - 3)
        for y in range(2):
            u22[x, y] = m * gathered(2 * x + y, 2, 1, y > 0, y < 1)
            u12[x, y] = pp[2 * x + y, pl.ds(SM, N), :]
    loop(5, lambda i: sum_u22(i + 1))
    last_own(wl, 448, load_u22, 2, 3)
    last_edges(wl, load_u22, 1, 5)

    def sum_e2(x):
        m = present(x - 3)
        for y in range(2):
            e2[x - 2, y] = m * (u12[x, y] + gathered(2 * x + y, 2, 1, y > 0, y < 1))
    loop(3, lambda i: sum_e2(i + 2))

    receive_all(u21_moves, s_u21, r_u21)

    def prolong(load):
        pair = jnp.concatenate([split(load(0)), split(load(1))], axis=1)
        out = jnp.dot(wp[...], pair, preferred_element_type=F32)
        return lambda at, child: out[N * child:N * (child + 1), LANES * at:LANES * (at + 1)]

    for i, (s, dst, dx, dy) in enumerate(u21_moves):
        @pl.when(inside(dx, dy))
        def _():
            remote(s, dst, s_u21.at[i], r_u21.at[i], dx, dy).wait_send()

    def lift1(x2):
        part = prolong(lambda y: e2[x2, y])
        for y2 in range(2):
            for child in range(4):
                x, y = 2 * x2 + child // 2, 2 * y2 + child % 2
                u21[x, y] = u21[x, y] + part(y2, child)
    loop(3, lift1)
    coarse_own(wl, 448, load_u21, 1, 4)
    coarse_edges(wl, load_u21, 0, 5)

    def sum_e1(x):
        m = present(device_of(x))
        for y in range(4):
            e1[x - 1, 1 + y] = m * (u11[x, y] + gathered(4 * x + y, 4, 1, y > 0, y < 3))
    loop(4, lambda i: sum_e1(i + 1))

    for i, (s, dst, dx, dy) in enumerate(u2_faces):
        @pl.when(inside(dx, dy))
        def _():
            remote(s, dst, s_u2.at[i], r_u2.at[i], dx, dy).wait_send()
    receive_all(u2_more, s_u2b, r_u2b)
    for i, (s, dst, dx, dy) in enumerate(u2_more):
        @pl.when(inside(dx, dy))
        def _():
            remote(s, dst, s_u2b.at[i], r_u2b.at[i], dx, dy).wait_send()

    wanted = {(y, x) for y in range(-2, 4) for x in range(-2, 6)
              if max(0, -y, y - 1) + max(0, -x, x - 3) <= 2}
    for j in range(3):
        for xp in range(2):
            part = prolong(lambda i: e1[2 * xp + i, gy + j])
            for i in range(2):
                for child in range(4):
                    x = 2 * (2 * xp + i - 1) + child // 2
                    y = 2 * (j - 1) + child % 2
                    if (y, x) in wanted:
                        u2[2 + y, 2 + x] = u2[2 + y, 2 + x] + part(i, child)

    def load_u2(c):
        return u2[2 + c[0], 2 + c[1]]

    def both(w, row, rows, c, e):
        apply(w, row, rows, load_u2, (c, e), (fine_at(*c), fine_at(*e)))

    def rows_wide(i):
        y, x = i // 3, (i % 3) * 2 - 1
        both(wl, 0, 448, (y, x), (y, x + 1))
    loop(6, rows_wide)

    def rows_short(i):
        y, x = (i // 2) * 3 - 1, (i % 2) * 2
        both(wl, 0, 448, (y, x), (y, x + 1))
    loop(4, rows_short)
    loop(2, lambda y: both(wl, XM, 128, (y, -2), (y, 5)))
    loop(4, lambda x: both(wl, YM, 128, (-2, x), (3, x)))
    loop(2, lambda i: both(wl, 0, 256, (3 * i - 1, -1), (3 * i - 1, 4)))

    def sum_u3(y, x, m=None):
        v = u1[1 + y, 1 + x] + gathered(fine_at(y, x), 1, 8)
        u3[1 + y, 1 + x] = v if m is None else m * v
        return v

    def own_u3(i):
        y, x = i // 4, i % 4
        v = sum_u3(y, x)
        sol[pl.ds(x * 2 + y, N, stride=8), :] = v
    loop(8, own_u3)
    loop(2, lambda y: sum_u3(y, -1, present(-1)))
    loop(2, lambda y: sum_u3(y, 4, present(1)))
    loop(4, lambda x: sum_u3(-1, x, keep(gy > 0)))
    loop(4, lambda x: sum_u3(2, x, keep(gy < ngy - 1)))
    fine_own(wb, 448, u3, 1, 1)
    fine_edges(wb, u3, 1, 1)

    def final(i):
        y, x = i // 4, i % 4
        c = x * 2 + y
        t = gathered(fine_at(y, x), 1, 8)
        res[pl.ds(c, N, stride=8), :] = src[pl.ds(c, N, stride=8), :] - kap[pl.ds(c, 1), :] * t
    loop(8, final)

    for group, ssem, rsem in ((q0_faces, s_q0, r_q0), (q2_moves, s_q2, r_q2)):
        for i, (s, dst, dx, dy) in enumerate(group):
            @pl.when(inside(dx, dy))
            def _():
                remote(s, dst, ssem.at[i], rsem.at[i], dx, dy).wait_send()
    for j in range(ngy):
        block = q1.at[pl.ds(2, 2), j]

        @pl.when(gy != j)
        def _():
            pltpu.make_async_remote_copy(
                src_ref=block, dst_ref=block, send_sem=s_g.at[j], recv_sem=r_g.at[j],
                device_id=(gx, j), device_id_type=MESH).wait_send()
        for i, (dx, at) in enumerate(((1, 0), (-1, 4))):
            @pl.when(inside(dx, 0))
            def _():
                remote(block, q1.at[pl.ds(at, 2), j], s_rl.at[i, j], r_rl.at[i, j], dx, 0).wait_send()


def solution(mesh):
    ngx, ngy = mesh.shape["gx"], mesh.shape["gy"]

    def shards(source, conductivity, diag_block, face_blocks, smoother, prolong):
        dma = pltpu.SemaphoreType.DMA
        col = (N, LANES)
        scratch = [
            pltpu.VMEM((4, 6) + col, F32),
            pltpu.VMEM((4, 6) + col, F32),
            pltpu.VMEM((6, 8) + col, F32),
            pltpu.VMEM((4, 6) + col, F32),
            pltpu.VMEM((6, 4, N + 8, LANES), F32),
            pltpu.VMEM((6, 4) + col, F32),
            pltpu.VMEM((6, 4) + col, F32),
            pltpu.VMEM((4, 6) + col, F32),
            pltpu.VMEM((7, 2) + col, F32),
            pltpu.VMEM((7, 2) + col, F32),
            pltpu.VMEM((7, 2) + col, F32),
            pltpu.VMEM((3, 2) + col, F32),
            pltpu.VMEM((48, 512, LANES), F32),
            pltpu.VMEM((8, 192, LANES), BF16),
            pltpu.VMEM((512, 192), BF16),
            pltpu.VMEM((448, 192), BF16),
            pltpu.VMEM((448, 192), BF16),
            pltpu.VMEM((256, 192), BF16),
            pltpu.VMEM((256, 192), BF16),
            dma((4,)), dma((4,)), dma((4,)), dma((4,)), dma((8,)), dma((8,)),
            dma((4,)), dma((4,)), dma((2, 4)), dma((2, 4)), dma((6,)), dma((6,)), dma((2,)), dma((2,)),
        ]
        shape = source.shape
        flat = jax.ShapeDtypeStruct((N * 8, LANES), F32)
        vmem = pl.BlockSpec(memory_space=pltpu.VMEM)
        sol, res = pl.pallas_call(
            functools.partial(kernel, ngx, ngy),
            out_shape=(flat, flat),
            in_specs=[vmem] * 6,
            out_specs=(vmem, vmem),
            scratch_shapes=scratch,
            compiler_params=pltpu.CompilerParams(
                collective_id=0, has_side_effects=True, vmem_limit_bytes=40 << 20),
            cost_estimate=pl.CostEstimate(flops=10**9, bytes_accessed=10**6, transcendentals=0),
        )(source.reshape(N * 8, LANES), conductivity.reshape(8, LANES),
          diag_block, face_blocks, smoother, prolong)
        return sol.reshape(shape), res.reshape(shape)

    return jax.shard_map(
        shards,
        mesh=mesh,
        in_specs=(P(None, "gx", "gy", None), P("gx", "gy", None), P(), P(), P(), P()),
        out_specs=(P(None, "gx", "gy", None), P(None, "gx", "gy", None)),
        check_vma=False,
    )
```

```python
import functools

import jax
import jax.numpy as jnp
from jax import lax
from jax.experimental import pallas as pl
from jax.experimental.pallas import tpu as pltpu
from jax.sharding import PartitionSpec as P

MESH = pl.DeviceIdType.MESH
F32 = jnp.float32
BF16 = jnp.bfloat16
OMEGA = 0.8
N = 64
LANES = 128
XM, XP, YM, YP, CC, ZM, ZP, SM = (64 * i for i in range(8))
FACES = (XM, XP, YM, YP, ZM, ZP)


def split(v):
    hi = v.astype(BF16)
    lo = (v - hi.astype(F32)).astype(BF16)
    return jnp.concatenate([hi, lo, hi], axis=0)


def exact_dot(a, b):
    return jnp.dot(a, b, precision=lax.Precision.HIGHEST, preferred_element_type=F32)


def widen(w):
    hi = w.astype(BF16)
    lo = (w - hi.astype(F32)).astype(BF16)
    return jnp.concatenate([hi, hi, lo], axis=1)


def kernel(ngx, ngy, src_h, kap_h, diag_h, faces_h, smooth_h, prol_h, both_out,
           src, kap, diag, faces, smooth, prol, s_in, q0, u1, u2, u3, q1, u11, u21, e1, q2, u12, u22, e2, pp, pb, rr,
           wm, wl, wb, wr, wp,
           s_q0, r_q0, s_qx, r_qx, s_qc, r_qc, s_u2b, r_u2b, s_g, r_g, s_rl, r_rl, s_q2, r_q2, s_u21, r_u21):
    sol, res = both_out.at[pl.ds(0, N * 8)], both_out.at[pl.ds(N * 8, N * 8)]
    gx, gy = lax.axis_index("gx"), lax.axis_index("gy")

    def inside(dx, dy):
        ok = None
        for at, d, n in ((gx, dx, ngx), (gy, dy, ngy)):
            if d:
                c = (at + d >= 0) & (at + d < n)
                ok = c if ok is None else ok & c
        return ok

    fetches = [pltpu.make_async_copy(a, b, s_in.at[i]) for i, (a, b) in enumerate((
        (src_h, src), (kap_h, kap), (smooth_h, smooth), (faces_h, faces), (diag_h, diag), (prol_h, prol)))]
    for f in fetches:
        f.start()

    barrier = pltpu.get_barrier_semaphore()
    partners = [(d, 0) for d in (-3, -2, -1, 1, 2, 3)] + [(0, d) for d in (-3, -2, -1, 1, 2, 3)]
    partners += [(a, b) for a in (-1, 1) for b in (-1, 1)]
    for dx, dy in partners:
        @pl.when(inside(dx, dy))
        def _():
            pl.semaphore_signal(barrier, inc=1, device_id=(gx + dx, gy + dy), device_id_type=MESH)
    fetches[1].wait()
    fetches[0].wait()
    for y in range(2):
        for x in range(4):
            c = x * 2 + y
            q0[2 + y, 2 + x] = src[pl.ds(c, N, stride=8), :] / kap[pl.ds(c, 1), :]
    peers = 0
    for dx, dy in partners:
        peers = peers + inside(dx, dy).astype(jnp.int32)
    pl.semaphore_wait(barrier, peers)

    def remote(s, d, ssem, rsem, dx, dy):
        return pltpu.make_async_remote_copy(
            src_ref=s, dst_ref=d, send_sem=ssem, recv_sem=rsem,
            device_id=(gx + dx, gy + dy), device_id_type=MESH)

    def send(s, d, ssem, rsem, dx, dy, cond=None):
        ok = inside(dx, dy) if cond is None else cond

        @pl.when(ok)
        def _():
            remote(s, d, ssem, rsem, dx, dy).start()

    def receive(d, ssem, rsem, dx, dy, cond=None):
        ok = inside(dx, dy) if cond is None else cond

        @pl.when(ok)
        def _():
            remote(d, d, ssem, rsem, dx, dy).wait_recv()

    def clear(ref, dx, dy):
        @pl.when(jnp.logical_not(inside(dx, dy)))
        def _():
            ref[...] = jnp.zeros(ref.shape, F32)

    def faces_x(buf):
        return [
            (buf.at[pl.ds(2, 2), 5], buf.at[pl.ds(2, 2), 1], 1, 0),
            (buf.at[pl.ds(2, 2), 2], buf.at[pl.ds(2, 2), 6], -1, 0),
            (buf.at[pl.ds(2, 2), 4], buf.at[pl.ds(2, 2), 0], 1, 0),
            (buf.at[pl.ds(2, 2), 3], buf.at[pl.ds(2, 2), 7], -1, 0),
        ]

    def near_y(buf, x, n):
        return [
            (buf.at[3, pl.ds(x, n)], buf.at[1, pl.ds(x, n)], 0, 1),
            (buf.at[2, pl.ds(x, n)], buf.at[4, pl.ds(x, n)], 0, -1),
        ]

    def far_y(buf, x, n):
        return [
            (buf.at[2, pl.ds(x, n)], buf.at[0, pl.ds(x, n)], 0, 1),
            (buf.at[3, pl.ds(x, n)], buf.at[5, pl.ds(x, n)], 0, -1),
        ]

    def corners(buf):
        return [
            (buf.at[3, 5], buf.at[1, 1], 1, 1),
            (buf.at[3, 2], buf.at[1, 6], -1, 1),
            (buf.at[2, 5], buf.at[4, 1], 1, -1),
            (buf.at[2, 2], buf.at[4, 6], -1, -1),
        ]

    def send_all(faces_of, ssem, rsem):
        for i, (s, d, dx, dy) in enumerate(faces_of):
            send(s, d, ssem.at[i], rsem.at[i], dx, dy)

    def receive_all(faces_of, ssem, rsem):
        for i, (s, d, dx, dy) in enumerate(faces_of):
            receive(d, ssem.at[i], rsem.at[i], -dx, -dy)

    q0_y = near_y(q0, 2, 1) + near_y(q0, 5, 1) + near_y(q0, 3, 2) + far_y(q0, 2, 2) + far_y(q0, 4, 2)
    q0_x = faces_x(q0)
    q0_c = [
        (q0.at[1, 5], q0.at[1, 1], 1, -1),
        (q0.at[4, 5], q0.at[4, 1], 1, 1),
        (q0.at[1, 2], q0.at[1, 6], -1, -1),
        (q0.at[4, 2], q0.at[4, 6], -1, 1),
    ]
    u2_more = far_y(u2, 2, 4) + faces_x(u2)[2:] + corners(u2)
    send_all(q0_y, s_q0, r_q0)
    send_all(q0_x, s_qx, r_qx)

    for f in fetches[2:]:
        f.wait()
    s8 = OMEGA * smooth[...]
    eye = (lax.broadcasted_iota(jnp.int32, (N, N), 0) == lax.broadcasted_iota(jnp.int32, (N, N), 1)).astype(F32)
    wm[pl.ds(SM, N), :] = widen(s8)
    for i, at in enumerate(FACES):
        f = faces[i]
        wb[pl.ds(at, N), :] = widen(-f)
        sf = exact_dot(s8, f)
        wl[pl.ds(at, N), :] = widen(sf)
        wm[pl.ds(at, N), :] = widen(exact_dot(sf, s8))
    d = diag[...]
    wb[pl.ds(CC, N), :] = widen(d)
    lc = eye - exact_dot(s8, d)
    wl[pl.ds(CC, N), :] = widen(lc)
    wm[pl.ds(CC, N), :] = widen(s8 + exact_dot(lc, s8))
    for i in range(4):
        p = prol[i]
        wp[pl.ds(N * i, N), :] = widen(p)
        wr[pl.ds(N * i, N), :] = widen(0.25 * p.T)

    for group in (q0_y, q0_x, u2_more):
        for _, dst, dx, dy in group:
            clear(dst, -dx, -dy)
    for _, dst, dx, dy in q0_c:
        clear(dst, -dx, dy)
    clear(q1.at[pl.ds(0, 2)], -1, 0)
    clear(q1.at[pl.ds(4, 2)], 1, 0)
    clear(u21.at[0], -1, 0)
    clear(u21.at[5], 1, 0)
    for dd in (1, 2, 3):
        clear(q2.at[3 - dd], -dd, 0)
        clear(q2.at[3 + dd], dd, 0)
    e1[:, 0] = jnp.zeros((4, N, LANES), F32)
    e1[:, 5] = jnp.zeros((4, N, LANES), F32)

    lane = lax.broadcasted_iota(jnp.int32, (N, LANES), 1)
    not_first, not_last = lane > 0, lane < LANES - 1

    def apply(w, row, rows, load, cols, at, to=pp):
        pair = jnp.concatenate([split(load(cols[0])), split(load(cols[1]))], axis=1)
        out = jnp.dot(w[pl.ds(row, rows), :], pair, preferred_element_type=F32)
        to[at[0], pl.ds(row, rows), :] = out[:, :LANES]
        to[at[1], pl.ds(row, rows), :] = out[:, LANES:]

    def gathered(c, sx, sy, ym=True, yp=True, of=pp):
        t = of[c, pl.ds(CC, N), :]
        t = t + of[c - sx, pl.ds(XM, N), :] + of[c + sx, pl.ds(XP, N), :]
        if ym:
            t = t + of[c - sy, pl.ds(YM, N), :]
        if yp:
            t = t + of[c + sy, pl.ds(YP, N), :]
        t = t + jnp.where(not_first, pltpu.roll(of[c, pl.ds(ZM, N), :], 1, 1), 0.0)
        t = t + jnp.where(not_last, pltpu.roll(of[c, pl.ds(ZP, N), :], LANES - 1, 1), 0.0)
        return t

    def loop(n, body):
        for i in range(n):
            body(i)

    def fine_at(y, x):
        return (y + 2) * 8 + x + 2

    def fine(w, row, rows, buf, c, e, to=pp):
        apply(w, row, rows, lambda p: buf[2 + p[0], 2 + p[1]], (c, e), (fine_at(*c), fine_at(*e)), to)

    def fine_own(w, rows, buf, to=pp):
        for y in range(2):
            for x in (0, 2):
                fine(w, 0, rows, buf, (y, x), (y, x + 1), to)

    def keep(ok):
        return jnp.where(ok, 1.0, 0.0).astype(F32)

    def present(offset):
        return keep((gx + offset >= 0) & (gx + offset < ngx))

    def side(offset):
        return keep((gy + offset >= 0) & (gy + offset < ngy))

    def take_u2(y, x, m=None):
        c = fine_at(y, x)
        v = gathered(c, 1, 8)
        u2[2 + y, 2 + x] = v if m is None else m * v
        u1[1 + y, 1 + x] = pp[c, pl.ds(SM, N), :]

    fine_own(wm, 512, q0)
    receive_all(q0_x, s_qx, r_qx)
    for y in range(2):
        fine(wm, 0, 512, q0, (y, -1), (y, 4))
        fine(wm, XM, 128, q0, (y, -2), (y, 5))

    def forward(group):
        for i, (s, d, dx, dy) in group:
            @pl.when(inside(dx, 0) & inside(0, dy))
            def _():
                pltpu.make_async_remote_copy(
                    src_ref=s, dst_ref=d, send_sem=s_qc.at[i], recv_sem=r_qc.at[i],
                    device_id=(gx + dx, gy), device_id_type=MESH).start()

    def receive_part(first, n):
        for i in range(first, first + n):
            s, d, dx, dy = q0_y[i]
            receive(d, s_q0.at[i], r_q0.at[i], -dx, -dy)

    receive_part(2, 2)
    forward([(0, q0_c[0]), (1, q0_c[1])])
    receive_part(0, 2)
    forward([(2, q0_c[2]), (3, q0_c[3])])
    receive_part(4, 2)
    for x in range(4):
        fine(wm, 0, 512, q0, (-1, x), (2, x))
    for y in range(2):
        for x in range(4):
            take_u2(y, x)
    fine_own(wb, 448, u2, pb)
    for i, (s, d, dx, dy) in enumerate(q0_c):
        @pl.when(inside(-dx, 0) & inside(0, dy))
        def _():
            pltpu.make_async_remote_copy(
                src_ref=d, dst_ref=d, send_sem=s_qc.at[i], recv_sem=r_qc.at[i],
                device_id=(gx - dx, gy), device_id_type=MESH).wait_recv()
    for y in (-1, 2):
        fine(wm, 0, 256, q0, (y, -1), (y, 4))
    for y in range(2):
        take_u2(y, -1, present(-1))
        take_u2(y, 4, present(1))
        fine(wb, XM, 128, u2, (y, -1), (y, 4), pb)

    def relay(j, at):
        for i, (dx, to) in enumerate(((1, 0), (-1, 4))):
            @pl.when(inside(dx, 0))
            def _():
                remote(q1.at[2 + at, j], q1.at[to + at, j], s_rl.at[i, at, j], r_rl.at[i, at, j], dx, 0).start()

    def half(at):
        receive_part(6 + 2 * at, 2)
        for x in (2 * at, 2 * at + 1):
            fine(wm, YM, 128, q0, (-2, x), (3, x))
        for x in (2 * at, 2 * at + 1):
            take_u2(-1, x, side(-1))
            take_u2(2, x, side(1))
        for x in (2 * at, 2 * at + 1):
            fine(wb, YM, 128, u2, (-1, x), (2, x), pb)
        total = None
        for x in (2 * at, 2 * at + 1):
            for y in range(2):
                t = gathered(fine_at(y, x), 1, 8, of=pb)
                k = kap[pl.ds(x * 2 + y, 1), :]
                r = split((q0[2 + y, 2 + x] - t) * k)
                child = 2 * (x - 2 * at) + y
                part = jnp.dot(wr[pl.ds(N * child, N), :], r, preferred_element_type=F32)
                total = part if total is None else total + part
        k1 = kap[pl.ds(4 * at, 1), :] + kap[pl.ds(4 * at + 1, 1), :]
        k1 = (k1 + (kap[pl.ds(4 * at + 2, 1), :] + kap[pl.ds(4 * at + 3, 1), :])) * 0.25
        q1[2 + at, gy, pl.ds(0, N), :] = total / k1
        q1[2 + at, gy, pl.ds(N, 8), :] = jnp.broadcast_to(k1, (8, LANES))
        for j in range(ngy):
            @pl.when(gy != j)
            def _():
                pltpu.make_async_remote_copy(
                    src_ref=q1.at[2 + at, gy], dst_ref=q1.at[2 + at, gy],
                    send_sem=s_g.at[at, j], recv_sem=r_g.at[at, gy],
                    device_id=(gx, j), device_id_type=MESH).start()
        relay(gy, at)

    half(0)
    half(1)

    def restrict(index):
        total = None
        for child in range(4):
            pair = jnp.concatenate([rr[index(0, child)], rr[index(1, child)]], axis=1)
            part = jnp.dot(wr[pl.ds(N * child, N), :], pair, preferred_element_type=F32)
            total = part if total is None else total + part
        return total[:, :LANES], total[:, LANES:]

    def arrive(j, at):
        block = q1.at[2 + at, j]
        pltpu.make_async_remote_copy(
            src_ref=block, dst_ref=block, send_sem=s_g.at[at, j], recv_sem=r_g.at[at, j],
            device_id=(gx, j), device_id_type=MESH).wait_recv()
        relay(j, at)
    for at in range(2):
        for dd in (1, -1, 2, -2, 3, -3):
            @pl.when(inside(0, dd))
            def _():
                arrive(gy + dd, at)
    send_all(u2_more, s_u2b, r_u2b)

    def coarse_own(w, rows, load, first, planes):
        def body(i):
            c = 4 * first + 2 * i
            apply(w, 0, rows, load, (c, c + 1), (c, c + 1))
        loop(2 * planes, body)

    def coarse_edges(w, load, low, high):
        def body(y):
            c, e = 4 * low + y, 4 * high + y
            apply(w, XM, 128, load, (c, e), (c, e))
        loop(4, body)

    def load_q1(c):
        return q1[c // 4, c % 4, pl.ds(0, N), :]

    def load_u21(c):
        return u21[c // 4, c % 4]

    coarse_own(wm, 512, load_q1, 2, 2)
    for at in range(2):
        for j in range(ngy):
            for i, (dx, to) in enumerate(((1, 0), (-1, 4))):
                @pl.when(inside(-dx, 0))
                def _():
                    block = q1.at[to + at, j]
                    remote(block, block, s_rl.at[i, at, j], r_rl.at[i, at, j], -dx, 0).wait_recv()
    coarse_own(wm, 512, load_q1, 1, 1)
    coarse_own(wm, 512, load_q1, 4, 1)
    coarse_edges(wm, load_q1, 0, 5)

    def device_of(x):
        return (x // 2) - 1

    def sum_u21(x):
        m = present(device_of(x))
        for y in range(4):
            c = 4 * x + y
            u21[x, y] = m * gathered(c, 4, 1, y > 0, y < 3)
            u11[x, y] = m * pp[c, pl.ds(SM, N), :]
    loop(4, lambda i: sum_u21(i + 1))

    u21_moves = [(u21.at[2], u21.at[0], 1, 0), (u21.at[3], u21.at[5], -1, 0)]
    send_all(u21_moves, s_u21, r_u21)
    coarse_own(wb, 448, load_u21, 2, 2)
    coarse_edges(wb, load_u21, 1, 4)

    def sum_r1(x):
        for y in range(4):
            t = gathered(4 * x + y, 4, 1, y > 0, y < 3)
            k1 = q1[x, y, pl.ds(N, 1), :]
            rr[(x - 2) * 4 + y] = split((q1[x, y, pl.ds(0, N), :] - t) * k1)
    loop(2, lambda i: sum_r1(i + 2))
    coarse2 = restrict(lambda at, child: (child // 2) * 4 + 2 * at + child % 2)
    for at in range(2):
        k2 = q1[2, 2 * at, pl.ds(N, 1), :] + q1[2, 2 * at + 1, pl.ds(N, 1), :]
        k2 = (k2 + (q1[3, 2 * at, pl.ds(N, 1), :] + q1[3, 2 * at + 1, pl.ds(N, 1), :])) * 0.25
        q2[3, at] = coarse2[at] / k2

    q2_moves = [(q2.at[3], q2.at[3 - dd], dd, 0) for dd in (1, -1, 2, -2, 3, -3)]
    send_all(q2_moves, s_q2, r_q2)

    def load_q2(c):
        return q2[c // 2, c % 2]

    def load_u22(c):
        return u22[c // 2, c % 2]

    def last_own(w, rows, load, first, planes):
        def body(i):
            c = 2 * first + 2 * i
            apply(w, 0, rows, load, (c, c + 1), (c, c + 1))
        loop(planes, body)

    def last_edges(w, load, low, high):
        def body(y):
            c, e = 2 * low + y, 2 * high + y
            apply(w, XM, 128, load, (c, e), (c, e))
        loop(2, body)

    last_own(wm, 512, load_q2, 3, 1)
    receive_all(q2_moves, s_q2, r_q2)
    last_own(wm, 512, load_q2, 1, 2)
    last_own(wm, 512, load_q2, 4, 2)
    last_edges(wm, load_q2, 0, 6)

    def sum_u22(x):
        m = present(x - 3)
        for y in range(2):
            u22[x, y] = m * gathered(2 * x + y, 2, 1, y > 0, y < 1)
            u12[x, y] = pp[2 * x + y, pl.ds(SM, N), :]
    loop(5, lambda i: sum_u22(i + 1))
    last_own(wl, 448, load_u22, 2, 3)
    last_edges(wl, load_u22, 1, 5)

    def sum_e2(x):
        m = present(x - 3)
        for y in range(2):
            e2[x - 2, y] = m * (u12[x, y] + gathered(2 * x + y, 2, 1, y > 0, y < 1))
    loop(3, lambda i: sum_e2(i + 2))

    receive_all(u21_moves, s_u21, r_u21)

    def prolong(load):
        pair = jnp.concatenate([split(load(0)), split(load(1))], axis=1)
        out = jnp.dot(wp[...], pair, preferred_element_type=F32)
        return lambda at, child: out[N * child:N * (child + 1), LANES * at:LANES * (at + 1)]

    for i, (s, dst, dx, dy) in enumerate(u21_moves):
        @pl.when(inside(dx, dy))
        def _():
            remote(s, dst, s_u21.at[i], r_u21.at[i], dx, dy).wait_send()

    def lift1(x2):
        part = prolong(lambda y: e2[x2, y])
        for y2 in range(2):
            for child in range(4):
                x, y = 2 * x2 + child // 2, 2 * y2 + child % 2
                u21[x, y] = u21[x, y] + part(y2, child)
    loop(3, lift1)
    coarse_own(wl, 448, load_u21, 1, 4)
    coarse_edges(wl, load_u21, 0, 5)

    def sum_e1(x):
        m = present(device_of(x))
        for y in range(4):
            e1[x - 1, 1 + y] = m * (u11[x, y] + gathered(4 * x + y, 4, 1, y > 0, y < 3))
    loop(4, lambda i: sum_e1(i + 1))

    receive_all(u2_more, s_u2b, r_u2b)
    for i, (s, dst, dx, dy) in enumerate(u2_more):
        @pl.when(inside(dx, dy))
        def _():
            remote(s, dst, s_u2b.at[i], r_u2b.at[i], dx, dy).wait_send()

    wanted = {(y, x) for y in range(-2, 4) for x in range(-2, 6)
              if max(0, -y, y - 1) + max(0, -x, x - 3) <= 2}
    for j in range(3):
        for xp in range(2):
            part = prolong(lambda i: e1[2 * xp + i, gy + j])
            for i in range(2):
                for child in range(4):
                    x = 2 * (2 * xp + i - 1) + child // 2
                    y = 2 * (j - 1) + child % 2
                    if (y, x) in wanted:
                        u2[2 + y, 2 + x] = u2[2 + y, 2 + x] + part(i, child)

    def load_u2(c):
        return u2[2 + c[0], 2 + c[1]]

    def both(w, row, rows, c, e):
        apply(w, row, rows, load_u2, (c, e), (fine_at(*c), fine_at(*e)))

    def rows_wide(i):
        y, x = i // 3, (i % 3) * 2 - 1
        both(wl, 0, 448, (y, x), (y, x + 1))
    loop(6, rows_wide)

    def rows_short(i):
        y, x = (i // 2) * 3 - 1, (i % 2) * 2
        both(wl, 0, 448, (y, x), (y, x + 1))
    loop(4, rows_short)
    loop(2, lambda y: both(wl, XM, 128, (y, -2), (y, 5)))
    loop(4, lambda x: both(wl, YM, 128, (-2, x), (3, x)))
    loop(2, lambda i: both(wl, 0, 256, (3 * i - 1, -1), (3 * i - 1, 4)))

    def sum_u3(y, x, m=None):
        v = u1[1 + y, 1 + x] + gathered(fine_at(y, x), 1, 8)
        u3[2 + y, 2 + x] = v if m is None else m * v
        return v

    def own_u3(i):
        y, x = i // 4, i % 4
        v = sum_u3(y, x)
        sol[pl.ds(x * 2 + y, N, stride=8), :] = v
    loop(8, own_u3)
    loop(2, lambda y: sum_u3(y, -1, present(-1)))
    loop(2, lambda y: sum_u3(y, 4, present(1)))
    loop(4, lambda x: sum_u3(-1, x, keep(gy > 0)))
    loop(4, lambda x: sum_u3(2, x, keep(gy < ngy - 1)))
    fine_own(wb, 448, u3)
    for y in range(2):
        fine(wb, XM, 128, u3, (y, -1), (y, 4))
    for x in range(4):
        fine(wb, YM, 128, u3, (-1, x), (2, x))

    def final(i):
        y, x = i // 4, i % 4
        c = x * 2 + y
        t = gathered(fine_at(y, x), 1, 8)
        res[pl.ds(c, N, stride=8), :] = src[pl.ds(c, N, stride=8), :] - kap[pl.ds(c, 1), :] * t
    loop(8, final)

    for group, ssem, rsem in ((q0_y, s_q0, r_q0), (q0_x, s_qx, r_qx), (q2_moves, s_q2, r_q2)):
        for i, (s, dst, dx, dy) in enumerate(group):
            @pl.when(inside(dx, dy))
            def _():
                remote(s, dst, ssem.at[i], rsem.at[i], dx, dy).wait_send()
    for i, (s, d, dx, dy) in enumerate(q0_c):
        @pl.when(inside(dx, 0) & inside(0, dy))
        def _():
            pltpu.make_async_remote_copy(
                src_ref=s, dst_ref=d, send_sem=s_qc.at[i], recv_sem=r_qc.at[i],
                device_id=(gx + dx, gy), device_id_type=MESH).wait_send()
    for at in range(2):
        for j in range(ngy):
            block = q1.at[2 + at, j]

            @pl.when(gy != j)
            def _():
                pltpu.make_async_remote_copy(
                    src_ref=block, dst_ref=block, send_sem=s_g.at[at, j], recv_sem=r_g.at[at, j],
                    device_id=(gx, j), device_id_type=MESH).wait_send()
            for i, (dx, to) in enumerate(((1, 0), (-1, 4))):
                @pl.when(inside(dx, 0))
                def _():
                    remote(block, q1.at[to + at, j], s_rl.at[i, at, j], r_rl.at[i, at, j], dx, 0).wait_send()


def solution(mesh):
    ngx, ngy = mesh.shape["gx"], mesh.shape["gy"]

    def shards(source, conductivity, diag_block, face_blocks, smoother, prolong):
        dma = pltpu.SemaphoreType.DMA
        col = (N, LANES)
        scratch = [
            pltpu.VMEM((N * 8, LANES), F32),
            pltpu.VMEM((8, LANES), F32),
            pltpu.VMEM((N, N), F32),
            pltpu.VMEM((6, N, N), F32),
            pltpu.VMEM((N, N), F32),
            pltpu.VMEM((4, N, N), F32),
            dma((6,)),
            pltpu.VMEM((6, 8) + col, F32),
            pltpu.VMEM((4, 6) + col, F32),
            pltpu.VMEM((6, 8) + col, F32),
            pltpu.VMEM((6, 8) + col, F32),
            pltpu.VMEM((6, 4, N + 8, LANES), F32),
            pltpu.VMEM((6, 4) + col, F32),
            pltpu.VMEM((6, 4) + col, F32),
            pltpu.VMEM((4, 6) + col, F32),
            pltpu.VMEM((7, 2) + col, F32),
            pltpu.VMEM((7, 2) + col, F32),
            pltpu.VMEM((7, 2) + col, F32),
            pltpu.VMEM((3, 2) + col, F32),
            pltpu.VMEM((48, 512, LANES), F32),
            pltpu.VMEM((48, 448, LANES), F32),
            pltpu.VMEM((8, 192, LANES), BF16),
            pltpu.VMEM((512, 192), BF16),
            pltpu.VMEM((448, 192), BF16),
            pltpu.VMEM((448, 192), BF16),
            pltpu.VMEM((256, 192), BF16),
            pltpu.VMEM((256, 192), BF16),
            dma((10,)), dma((10,)), dma((4,)), dma((4,)), dma((4,)), dma((4,)), dma((8,)), dma((8,)),
            dma((2, 4)), dma((2, 4)), dma((2, 2, 4)), dma((2, 2, 4)), dma((6,)), dma((6,)), dma((2,)), dma((2,)),
        ]
        shape = source.shape
        flat = jax.ShapeDtypeStruct((2 * N * 8, LANES), F32)
        vmem = pl.BlockSpec(memory_space=pltpu.VMEM)
        both = pl.pallas_call(
            functools.partial(kernel, ngx, ngy),
            out_shape=flat,
            in_specs=[pl.BlockSpec(memory_space=pl.ANY)] * 6,
            out_specs=vmem,
            scratch_shapes=scratch,
            compiler_params=pltpu.CompilerParams(
                collective_id=0, has_side_effects=True, vmem_limit_bytes=60 << 20),
            cost_estimate=pl.CostEstimate(flops=10**9, bytes_accessed=10**6, transcendentals=0),
        )(source.reshape(N * 8, LANES), conductivity.reshape(8, LANES),
          diag_block, face_blocks, smoother, prolong)
        return both[:N * 8].reshape(shape), both[N * 8:].reshape(shape)

    return jax.shard_map(
        shards,
        mesh=mesh,
        in_specs=(P(None, "gx", "gy", None), P("gx", "gy", None), P(), P(), P(), P()),
        out_specs=(P(None, "gx", "gy", None), P(None, "gx", "gy", None)),
        check_vma=False,
    )
```

```python
import functools

import jax
import jax.numpy as jnp
from jax import lax
from jax.experimental import pallas as pl
from jax.experimental.pallas import tpu as pltpu
from jax.sharding import PartitionSpec as P

MESH = pl.DeviceIdType.MESH
F32 = jnp.float32
BF16 = jnp.bfloat16
OMEGA = 0.8
N = 64
LANES = 128
XM, XP, YM, YP, CC, ZM, ZP, SM = (64 * i for i in range(8))
FACES = (XM, XP, YM, YP, ZM, ZP)


def split(v):
    hi = v.astype(BF16)
    lo = (v - hi.astype(F32)).astype(BF16)
    return jnp.concatenate([hi, lo, hi], axis=0)


def exact_dot(a, b):
    return jnp.dot(a, b, precision=lax.Precision.HIGHEST, preferred_element_type=F32)


def widen(w):
    hi = w.astype(BF16)
    lo = (w - hi.astype(F32)).astype(BF16)
    return jnp.concatenate([hi, hi, lo], axis=1)


def kernel(ngx, ngy, src_h, kap_h, diag_h, faces_h, smooth_h, prol_h, both_out,
           held, s_out, src, kap, diag, faces, smooth, prol, s_in, q0, u1, u2, u3, q1, u11, u21, e1, q2, u12, u22, e2, pp, pb, rr,
           wm, wl, wb, wr, wp,
           s_q0, r_q0, s_qx, r_qx, s_qc, r_qc, s_u2b, r_u2b, s_g, r_g, s_rl, r_rl, s_q2, r_q2, s_u21, r_u21):
    sol, res = held.at[0], held.at[1]

    def store(i):
        return pltpu.make_async_copy(held.at[i], both_out.at[pl.ds(N * 8 * i, N * 8)], s_out.at[i])

    gx, gy = lax.axis_index("gx"), lax.axis_index("gy")

    def inside(dx, dy):
        ok = None
        for at, d, n in ((gx, dx, ngx), (gy, dy, ngy)):
            if d:
                c = (at + d >= 0) & (at + d < n)
                ok = c if ok is None else ok & c
        return ok

    fetches = [pltpu.make_async_copy(a, b, s_in.at[i]) for i, (a, b) in enumerate((
        (src_h, src), (kap_h, kap), (smooth_h, smooth), (faces_h, faces), (diag_h, diag), (prol_h, prol)))]
    for f in fetches:
        f.start()

    barrier = pltpu.get_barrier_semaphore()
    partners = [(d, 0) for d in (-3, -2, -1, 1, 2, 3)] + [(0, d) for d in (-3, -2, -1, 1, 2, 3)]
    partners += [(a, b) for a in (-1, 1) for b in (-1, 1)]
    for dx, dy in partners:
        @pl.when(inside(dx, dy))
        def _():
            pl.semaphore_signal(barrier, inc=1, device_id=(gx + dx, gy + dy), device_id_type=MESH)
    fetches[1].wait()
    fetches[0].wait()
    for y in range(2):
        for x in range(4):
            c = x * 2 + y
            q0[2 + y, 2 + x] = src[pl.ds(c, N, stride=8), :] / kap[pl.ds(c, 1), :]
    peers = 0
    for dx, dy in partners:
        peers = peers + inside(dx, dy).astype(jnp.int32)
    pl.semaphore_wait(barrier, peers)

    def remote(s, d, ssem, rsem, dx, dy):
        return pltpu.make_async_remote_copy(
            src_ref=s, dst_ref=d, send_sem=ssem, recv_sem=rsem,
            device_id=(gx + dx, gy + dy), device_id_type=MESH)

    def send(s, d, ssem, rsem, dx, dy, cond=None):
        ok = inside(dx, dy) if cond is None else cond

        @pl.when(ok)
        def _():
            remote(s, d, ssem, rsem, dx, dy).start()

    def receive(d, ssem, rsem, dx, dy, cond=None):
        ok = inside(dx, dy) if cond is None else cond

        @pl.when(ok)
        def _():
            remote(d, d, ssem, rsem, dx, dy).wait_recv()

    def clear(ref, dx, dy):
        @pl.when(jnp.logical_not(inside(dx, dy)))
        def _():
            ref[...] = jnp.zeros(ref.shape, F32)

    def faces_x(buf):
        return [
            (buf.at[pl.ds(2, 2), 5], buf.at[pl.ds(2, 2), 1], 1, 0),
            (buf.at[pl.ds(2, 2), 2], buf.at[pl.ds(2, 2), 6], -1, 0),
            (buf.at[pl.ds(2, 2), 4], buf.at[pl.ds(2, 2), 0], 1, 0),
            (buf.at[pl.ds(2, 2), 3], buf.at[pl.ds(2, 2), 7], -1, 0),
        ]

    def near_y(buf, x, n):
        return [
            (buf.at[3, pl.ds(x, n)], buf.at[1, pl.ds(x, n)], 0, 1),
            (buf.at[2, pl.ds(x, n)], buf.at[4, pl.ds(x, n)], 0, -1),
        ]

    def far_y(buf, x, n):
        return [
            (buf.at[2, pl.ds(x, n)], buf.at[0, pl.ds(x, n)], 0, 1),
            (buf.at[3, pl.ds(x, n)], buf.at[5, pl.ds(x, n)], 0, -1),
        ]

    def corners(buf):
        return [
            (buf.at[3, 5], buf.at[1, 1], 1, 1),
            (buf.at[3, 2], buf.at[1, 6], -1, 1),
            (buf.at[2, 5], buf.at[4, 1], 1, -1),
            (buf.at[2, 2], buf.at[4, 6], -1, -1),
        ]

    def send_all(faces_of, ssem, rsem):
        for i, (s, d, dx, dy) in enumerate(faces_of):
            send(s, d, ssem.at[i], rsem.at[i], dx, dy)

    def receive_all(faces_of, ssem, rsem):
        for i, (s, d, dx, dy) in enumerate(faces_of):
            receive(d, ssem.at[i], rsem.at[i], -dx, -dy)

    q0_y = near_y(q0, 2, 1) + near_y(q0, 5, 1) + near_y(q0, 3, 2) + far_y(q0, 2, 2) + far_y(q0, 4, 2)
    q0_x = faces_x(q0)
    q0_c = [
        (q0.at[1, 5], q0.at[1, 1], 1, -1),
        (q0.at[4, 5], q0.at[4, 1], 1, 1),
        (q0.at[1, 2], q0.at[1, 6], -1, -1),
        (q0.at[4, 2], q0.at[4, 6], -1, 1),
    ]
    u2_more = far_y(u2, 2, 4) + faces_x(u2)[2:] + corners(u2)
    send_all(q0_y, s_q0, r_q0)
    send_all(q0_x, s_qx, r_qx)

    for f in fetches[2:]:
        f.wait()
    s8 = OMEGA * smooth[...]
    eye = (lax.broadcasted_iota(jnp.int32, (N, N), 0) == lax.broadcasted_iota(jnp.int32, (N, N), 1)).astype(F32)
    wm[pl.ds(SM, N), :] = widen(s8)
    for i, at in enumerate(FACES):
        f = faces[i]
        wb[pl.ds(at, N), :] = widen(-f)
        sf = exact_dot(s8, f)
        wl[pl.ds(at, N), :] = widen(sf)
        wm[pl.ds(at, N), :] = widen(exact_dot(sf, s8))
    d = diag[...]
    wb[pl.ds(CC, N), :] = widen(d)
    lc = eye - exact_dot(s8, d)
    wl[pl.ds(CC, N), :] = widen(lc)
    wm[pl.ds(CC, N), :] = widen(s8 + exact_dot(lc, s8))
    for i in range(4):
        p = prol[i]
        wp[pl.ds(N * i, N), :] = widen(p)
        wr[pl.ds(N * i, N), :] = widen(0.25 * p.T)

    for group in (q0_y, q0_x, u2_more):
        for _, dst, dx, dy in group:
            clear(dst, -dx, -dy)
    for _, dst, dx, dy in q0_c:
        clear(dst, -dx, dy)
    clear(q1.at[pl.ds(0, 2)], -1, 0)
    clear(q1.at[pl.ds(4, 2)], 1, 0)
    clear(u21.at[0], -1, 0)
    clear(u21.at[5], 1, 0)
    for dd in (1, 2, 3):
        clear(q2.at[3 - dd], -dd, 0)
        clear(q2.at[3 + dd], dd, 0)
    e1[:, 0] = jnp.zeros((4, N, LANES), F32)
    e1[:, 5] = jnp.zeros((4, N, LANES), F32)

    lane = lax.broadcasted_iota(jnp.int32, (N, LANES), 1)
    not_first, not_last = lane > 0, lane < LANES - 1

    def apply(w, row, rows, load, cols, at, to=pp):
        pair = jnp.concatenate([split(load(cols[0])), split(load(cols[1]))], axis=1)
        out = jnp.dot(w[pl.ds(row, rows), :], pair, preferred_element_type=F32)
        to[at[0], pl.ds(row, rows), :] = out[:, :LANES]
        to[at[1], pl.ds(row, rows), :] = out[:, LANES:]

    def gathered(c, sx, sy, ym=True, yp=True, of=pp):
        t = of[c, pl.ds(CC, N), :]
        t = t + of[c - sx, pl.ds(XM, N), :] + of[c + sx, pl.ds(XP, N), :]
        if ym:
            t = t + of[c - sy, pl.ds(YM, N), :]
        if yp:
            t = t + of[c + sy, pl.ds(YP, N), :]
        t = t + jnp.where(not_first, pltpu.roll(of[c, pl.ds(ZM, N), :], 1, 1), 0.0)
        t = t + jnp.where(not_last, pltpu.roll(of[c, pl.ds(ZP, N), :], LANES - 1, 1), 0.0)
        return t

    def loop(n, body):
        for i in range(n):
            body(i)

    def fine_at(y, x):
        return (y + 2) * 8 + x + 2

    def fine(w, row, rows, buf, c, e, to=pp):
        apply(w, row, rows, lambda p: buf[2 + p[0], 2 + p[1]], (c, e), (fine_at(*c), fine_at(*e)), to)

    def fine_own(w, rows, buf, to=pp):
        for y in range(2):
            for x in (0, 2):
                fine(w, 0, rows, buf, (y, x), (y, x + 1), to)

    def keep(ok):
        return jnp.where(ok, 1.0, 0.0).astype(F32)

    def present(offset):
        return keep((gx + offset >= 0) & (gx + offset < ngx))

    def side(offset):
        return keep((gy + offset >= 0) & (gy + offset < ngy))

    def take_u2(y, x, m=None):
        c = fine_at(y, x)
        v = gathered(c, 1, 8)
        u2[2 + y, 2 + x] = v if m is None else m * v
        u1[1 + y, 1 + x] = pp[c, pl.ds(SM, N), :]

    fine_own(wm, 512, q0)
    receive_all(q0_x, s_qx, r_qx)
    for y in range(2):
        fine(wm, 0, 512, q0, (y, -1), (y, 4))
        fine(wm, XM, 128, q0, (y, -2), (y, 5))

    def forward(group):
        for i, (s, d, dx, dy) in group:
            @pl.when(inside(dx, 0) & inside(0, dy))
            def _():
                pltpu.make_async_remote_copy(
                    src_ref=s, dst_ref=d, send_sem=s_qc.at[i], recv_sem=r_qc.at[i],
                    device_id=(gx + dx, gy), device_id_type=MESH).start()

    def receive_part(first, n):
        for i in range(first, first + n):
            s, d, dx, dy = q0_y[i]
            receive(d, s_q0.at[i], r_q0.at[i], -dx, -dy)

    receive_part(2, 2)
    forward([(0, q0_c[0]), (1, q0_c[1])])
    receive_part(0, 2)
    forward([(2, q0_c[2]), (3, q0_c[3])])
    receive_part(4, 2)
    for x in range(4):
        fine(wm, 0, 512, q0, (-1, x), (2, x))
    for y in range(2):
        for x in range(4):
            take_u2(y, x)
    fine_own(wb, 448, u2, pb)
    for i, (s, d, dx, dy) in enumerate(q0_c):
        @pl.when(inside(-dx, 0) & inside(0, dy))
        def _():
            pltpu.make_async_remote_copy(
                src_ref=d, dst_ref=d, send_sem=s_qc.at[i], recv_sem=r_qc.at[i],
                device_id=(gx - dx, gy), device_id_type=MESH).wait_recv()
    for y in (-1, 2):
        fine(wm, 0, 256, q0, (y, -1), (y, 4))
    for y in range(2):
        take_u2(y, -1, present(-1))
        take_u2(y, 4, present(1))
        fine(wb, XM, 128, u2, (y, -1), (y, 4), pb)

    def relay(j, at):
        for i, (dx, to) in enumerate(((1, 0), (-1, 4))):
            @pl.when(inside(dx, 0))
            def _():
                remote(q1.at[2 + at, j, pl.ds(0, N)], q1.at[to + at, j, pl.ds(0, N)], s_rl.at[i, at, j], r_rl.at[i, at, j], dx, 0).start()

    def half(at):
        receive_part(6 + 2 * at, 2)
        for x in (2 * at, 2 * at + 1):
            fine(wm, YM, 128, q0, (-2, x), (3, x))
        for x in (2 * at, 2 * at + 1):
            take_u2(-1, x, side(-1))
            take_u2(2, x, side(1))
        for x in (2 * at, 2 * at + 1):
            fine(wb, YM, 128, u2, (-1, x), (2, x), pb)
        total = None
        for x in (2 * at, 2 * at + 1):
            for y in range(2):
                t = gathered(fine_at(y, x), 1, 8, of=pb)
                k = kap[pl.ds(x * 2 + y, 1), :]
                r = split((q0[2 + y, 2 + x] - t) * k)
                child = 2 * (x - 2 * at) + y
                part = jnp.dot(wr[pl.ds(N * child, N), :], r, preferred_element_type=F32)
                total = part if total is None else total + part
        k1 = kap[pl.ds(4 * at, 1), :] + kap[pl.ds(4 * at + 1, 1), :]
        k1 = (k1 + (kap[pl.ds(4 * at + 2, 1), :] + kap[pl.ds(4 * at + 3, 1), :])) * 0.25
        q1[2 + at, gy, pl.ds(0, N), :] = total / k1
        q1[2 + at, gy, pl.ds(N, 8), :] = jnp.broadcast_to(k1, (8, LANES))
        for j in range(ngy):
            @pl.when(gy != j)
            def _():
                pltpu.make_async_remote_copy(
                    src_ref=q1.at[2 + at, gy], dst_ref=q1.at[2 + at, gy],
                    send_sem=s_g.at[at, j], recv_sem=r_g.at[at, gy],
                    device_id=(gx, j), device_id_type=MESH).start()
        relay(gy, at)

    half(0)
    half(1)

    def restrict(index):
        total = None
        for child in range(4):
            pair = jnp.concatenate([rr[index(0, child)], rr[index(1, child)]], axis=1)
            part = jnp.dot(wr[pl.ds(N * child, N), :], pair, preferred_element_type=F32)
            total = part if total is None else total + part
        return total[:, :LANES], total[:, LANES:]

    def arrive(j, at):
        block = q1.at[2 + at, j]
        pltpu.make_async_remote_copy(
            src_ref=block, dst_ref=block, send_sem=s_g.at[at, j], recv_sem=r_g.at[at, j],
            device_id=(gx, j), device_id_type=MESH).wait_recv()
        relay(j, at)
    for at in range(2):
        for dd in (1, -1, 2, -2, 3, -3):
            @pl.when(inside(0, dd))
            def _():
                arrive(gy + dd, at)
    send_all(u2_more, s_u2b, r_u2b)

    def coarse_own(w, rows, load, first, planes):
        def body(i):
            c = 4 * first + 2 * i
            apply(w, 0, rows, load, (c, c + 1), (c, c + 1))
        loop(2 * planes, body)

    def coarse_edges(w, load, low, high):
        def body(y):
            c, e = 4 * low + y, 4 * high + y
            apply(w, XM, 128, load, (c, e), (c, e))
        loop(4, body)

    def load_q1(c):
        return q1[c // 4, c % 4, pl.ds(0, N), :]

    def load_u21(c):
        return u21[c // 4, c % 4]

    coarse_own(wm, 512, load_q1, 2, 2)
    for at in range(2):
        for j in range(ngy):
            for i, (dx, to) in enumerate(((1, 0), (-1, 4))):
                @pl.when(inside(-dx, 0))
                def _():
                    block = q1.at[to + at, j, pl.ds(0, N)]
                    remote(block, block, s_rl.at[i, at, j], r_rl.at[i, at, j], -dx, 0).wait_recv()
    coarse_own(wm, 512, load_q1, 1, 1)
    coarse_own(wm, 512, load_q1, 4, 1)
    coarse_edges(wm, load_q1, 0, 5)

    def device_of(x):
        return (x // 2) - 1

    def sum_u21(x):
        m = present(device_of(x))
        for y in range(4):
            c = 4 * x + y
            u21[x, y] = m * gathered(c, 4, 1, y > 0, y < 3)
            u11[x, y] = m * pp[c, pl.ds(SM, N), :]
    loop(4, lambda i: sum_u21(i + 1))

    low = pl.ds(jnp.clip(gy - 1, 0, ngy - 3), 3)
    u21_moves = [(u21.at[2, low], u21.at[0, low], 1, 0), (u21.at[3, low], u21.at[5, low], -1, 0)]
    send_all(u21_moves, s_u21, r_u21)
    coarse_own(wb, 448, load_u21, 2, 2)
    coarse_edges(wb, load_u21, 1, 4)

    def sum_r1(x):
        for y in range(4):
            t = gathered(4 * x + y, 4, 1, y > 0, y < 3)
            k1 = q1[x, y, pl.ds(N, 1), :]
            rr[(x - 2) * 4 + y] = split((q1[x, y, pl.ds(0, N), :] - t) * k1)
    loop(2, lambda i: sum_r1(i + 2))
    coarse2 = restrict(lambda at, child: (child // 2) * 4 + 2 * at + child % 2)
    for at in range(2):
        k2 = q1[2, 2 * at, pl.ds(N, 1), :] + q1[2, 2 * at + 1, pl.ds(N, 1), :]
        k2 = (k2 + (q1[3, 2 * at, pl.ds(N, 1), :] + q1[3, 2 * at + 1, pl.ds(N, 1), :])) * 0.25
        q2[3, at] = coarse2[at] / k2

    q2_moves = [(q2.at[3], q2.at[3 - dd], dd, 0) for dd in (1, -1, 2, -2, 3, -3)]
    send_all(q2_moves, s_q2, r_q2)

    def load_q2(c):
        return q2[c // 2, c % 2]

    def load_u22(c):
        return u22[c // 2, c % 2]

    def last_own(w, rows, load, first, planes):
        def body(i):
            c = 2 * first + 2 * i
            apply(w, 0, rows, load, (c, c + 1), (c, c + 1))
        loop(planes, body)

    def last_edges(w, load, low, high):
        def body(y):
            c, e = 2 * low + y, 2 * high + y
            apply(w, XM, 128, load, (c, e), (c, e))
        loop(2, body)

    last_own(wm, 512, load_q2, 3, 1)
    for group, ssem, rsem in ((q0_y, s_q0, r_q0), (q0_x, s_qx, r_qx)):
        for i, (s, dst, dx, dy) in enumerate(group):
            @pl.when(inside(dx, dy))
            def _():
                remote(s, dst, ssem.at[i], rsem.at[i], dx, dy).wait_send()
    for i, (s, d, dx, dy) in enumerate(q0_c):
        @pl.when(inside(dx, 0) & inside(0, dy))
        def _():
            pltpu.make_async_remote_copy(
                src_ref=s, dst_ref=d, send_sem=s_qc.at[i], recv_sem=r_qc.at[i],
                device_id=(gx + dx, gy), device_id_type=MESH).wait_send()
    for at in range(2):
        for j in range(ngy):
            block = q1.at[2 + at, j]

            @pl.when(gy != j)
            def _():
                pltpu.make_async_remote_copy(
                    src_ref=block, dst_ref=block, send_sem=s_g.at[at, j], recv_sem=r_g.at[at, j],
                    device_id=(gx, j), device_id_type=MESH).wait_send()
            for i, (dx, to) in enumerate(((1, 0), (-1, 4))):
                @pl.when(inside(dx, 0))
                def _():
                    remote(block.at[pl.ds(0, N)], q1.at[to + at, j, pl.ds(0, N)], s_rl.at[i, at, j], r_rl.at[i, at, j], dx, 0).wait_send()
    receive_all(q2_moves, s_q2, r_q2)
    last_own(wm, 512, load_q2, 1, 2)
    last_own(wm, 512, load_q2, 4, 2)
    last_edges(wm, load_q2, 0, 6)

    def sum_u22(x):
        m = present(x - 3)
        for y in range(2):
            u22[x, y] = m * gathered(2 * x + y, 2, 1, y > 0, y < 1)
            u12[x, y] = pp[2 * x + y, pl.ds(SM, N), :]
    loop(5, lambda i: sum_u22(i + 1))
    last_own(wl, 448, load_u22, 2, 3)
    last_edges(wl, load_u22, 1, 5)

    def sum_e2(x):
        m = present(x - 3)
        for y in range(2):
            e2[x - 2, y] = m * (u12[x, y] + gathered(2 * x + y, 2, 1, y > 0, y < 1))
    loop(3, lambda i: sum_e2(i + 2))

    receive_all(u21_moves, s_u21, r_u21)

    def prolong(load):
        pair = jnp.concatenate([split(load(0)), split(load(1))], axis=1)
        out = jnp.dot(wp[...], pair, preferred_element_type=F32)
        return lambda at, child: out[N * child:N * (child + 1), LANES * at:LANES * (at + 1)]

    for i, (s, dst, dx, dy) in enumerate(q2_moves):
        @pl.when(inside(dx, dy))
        def _():
            remote(s, dst, s_q2.at[i], r_q2.at[i], dx, dy).wait_send()

    for i, (s, dst, dx, dy) in enumerate(u21_moves):
        @pl.when(inside(dx, dy))
        def _():
            remote(s, dst, s_u21.at[i], r_u21.at[i], dx, dy).wait_send()

    def lift1(x2):
        part = prolong(lambda y: e2[x2, y])
        for y2 in range(2):
            for child in range(4):
                x, y = 2 * x2 + child // 2, 2 * y2 + child % 2
                u21[x, y] = u21[x, y] + part(y2, child)
    loop(3, lift1)
    coarse_own(wl, 448, load_u21, 1, 4)
    coarse_edges(wl, load_u21, 0, 5)

    def sum_e1(x):
        m = present(device_of(x))
        for y in range(4):
            e1[x - 1, 1 + y] = m * (u11[x, y] + gathered(4 * x + y, 4, 1, y > 0, y < 3))
    loop(4, lambda i: sum_e1(i + 1))

    receive_all(u2_more, s_u2b, r_u2b)
    for i, (s, dst, dx, dy) in enumerate(u2_more):
        @pl.when(inside(dx, dy))
        def _():
            remote(s, dst, s_u2b.at[i], r_u2b.at[i], dx, dy).wait_send()

    wanted = {(y, x) for y in range(-2, 4) for x in range(-2, 6)
              if max(0, -y, y - 1) + max(0, -x, x - 3) <= 2}
    for j in range(3):
        for xp in range(2):
            part = prolong(lambda i: e1[2 * xp + i, gy + j])
            for i in range(2):
                for child in range(4):
                    x = 2 * (2 * xp + i - 1) + child // 2
                    y = 2 * (j - 1) + child % 2
                    if (y, x) in wanted:
                        u2[2 + y, 2 + x] = u2[2 + y, 2 + x] + part(i, child)

    def load_u2(c):
        return u2[2 + c[0], 2 + c[1]]

    def both(w, row, rows, c, e):
        apply(w, row, rows, load_u2, (c, e), (fine_at(*c), fine_at(*e)))

    def rows_wide(i):
        y, x = i // 3, (i % 3) * 2 - 1
        both(wl, 0, 448, (y, x), (y, x + 1))
    loop(6, rows_wide)

    def rows_short(i):
        y, x = (i // 2) * 3 - 1, (i % 2) * 2
        both(wl, 0, 448, (y, x), (y, x + 1))
    loop(4, rows_short)
    loop(2, lambda y: both(wl, XM, 128, (y, -2), (y, 5)))
    loop(4, lambda x: both(wl, YM, 128, (-2, x), (3, x)))
    loop(2, lambda i: both(wl, 0, 256, (3 * i - 1, -1), (3 * i - 1, 4)))

    def sum_u3(y, x, m=None):
        v = u1[1 + y, 1 + x] + gathered(fine_at(y, x), 1, 8)
        u3[2 + y, 2 + x] = v if m is None else m * v
        return v

    def own_u3(i):
        y, x = i // 4, i % 4
        v = sum_u3(y, x)
        sol[pl.ds(x * 2 + y, N, stride=8), :] = v
    loop(8, own_u3)
    store(0).start()
    loop(2, lambda y: sum_u3(y, -1, present(-1)))
    loop(2, lambda y: sum_u3(y, 4, present(1)))
    loop(4, lambda x: sum_u3(-1, x, keep(gy > 0)))
    loop(4, lambda x: sum_u3(2, x, keep(gy < ngy - 1)))
    fine_own(wb, 448, u3)
    for y in range(2):
        fine(wb, XM, 128, u3, (y, -1), (y, 4))
    for x in range(4):
        fine(wb, YM, 128, u3, (-1, x), (2, x))

    def final(i):
        y, x = i // 4, i % 4
        c = x * 2 + y
        t = gathered(fine_at(y, x), 1, 8)
        res[pl.ds(c, N, stride=8), :] = src[pl.ds(c, N, stride=8), :] - kap[pl.ds(c, 1), :] * t
    loop(8, final)
    store(1).start()

    store(0).wait()
    store(1).wait()


def solution(mesh):
    ngx, ngy = mesh.shape["gx"], mesh.shape["gy"]

    def shards(source, conductivity, diag_block, face_blocks, smoother, prolong):
        dma = pltpu.SemaphoreType.DMA
        col = (N, LANES)
        scratch = [
            pltpu.VMEM((2, N * 8, LANES), F32),
            dma((2,)),
            pltpu.VMEM((N * 8, LANES), F32),
            pltpu.VMEM((8, LANES), F32),
            pltpu.VMEM((N, N), F32),
            pltpu.VMEM((6, N, N), F32),
            pltpu.VMEM((N, N), F32),
            pltpu.VMEM((4, N, N), F32),
            dma((6,)),
            pltpu.VMEM((6, 8) + col, F32),
            pltpu.VMEM((4, 6) + col, F32),
            pltpu.VMEM((6, 8) + col, F32),
            pltpu.VMEM((6, 8) + col, F32),
            pltpu.VMEM((6, 4, N + 8, LANES), F32),
            pltpu.VMEM((6, 4) + col, F32),
            pltpu.VMEM((6, 4) + col, F32),
            pltpu.VMEM((4, 6) + col, F32),
            pltpu.VMEM((7, 2) + col, F32),
            pltpu.VMEM((7, 2) + col, F32),
            pltpu.VMEM((7, 2) + col, F32),
            pltpu.VMEM((3, 2) + col, F32),
            pltpu.VMEM((48, 512, LANES), F32),
            pltpu.VMEM((48, 448, LANES), F32),
            pltpu.VMEM((8, 192, LANES), BF16),
            pltpu.VMEM((512, 192), BF16),
            pltpu.VMEM((448, 192), BF16),
            pltpu.VMEM((448, 192), BF16),
            pltpu.VMEM((256, 192), BF16),
            pltpu.VMEM((256, 192), BF16),
            dma((10,)), dma((10,)), dma((4,)), dma((4,)), dma((4,)), dma((4,)), dma((8,)), dma((8,)),
            dma((2, 4)), dma((2, 4)), dma((2, 2, 4)), dma((2, 2, 4)), dma((6,)), dma((6,)), dma((2,)), dma((2,)),
        ]
        shape = source.shape
        flat = jax.ShapeDtypeStruct((2 * N * 8, LANES), F32)
        both = pl.pallas_call(
            functools.partial(kernel, ngx, ngy),
            out_shape=flat,
            in_specs=[pl.BlockSpec(memory_space=pl.ANY)] * 6,
            out_specs=pl.BlockSpec(memory_space=pl.ANY),
            scratch_shapes=scratch,
            compiler_params=pltpu.CompilerParams(
                collective_id=0, has_side_effects=True, vmem_limit_bytes=60 << 20),
            cost_estimate=pl.CostEstimate(flops=10**9, bytes_accessed=10**6, transcendentals=0),
        )(source.reshape(N * 8, LANES), conductivity.reshape(8, LANES),
          diag_block, face_blocks, smoother, prolong)
        return both[:N * 8].reshape(shape), both[N * 8:].reshape(shape)

    return jax.shard_map(
        shards,
        mesh=mesh,
        in_specs=(P(None, "gx", "gy", None), P("gx", "gy", None), P(), P(), P(), P()),
        out_specs=(P(None, "gx", "gy", None), P(None, "gx", "gy", None)),
        check_vma=False,
    )
```

```python
import functools

import jax
import jax.numpy as jnp
from jax import lax
from jax.experimental import pallas as pl
from jax.experimental.pallas import tpu as pltpu
from jax.sharding import PartitionSpec as P

MESH = pl.DeviceIdType.MESH
F32 = jnp.float32
BF16 = jnp.bfloat16
OMEGA = 0.8
N = 64
LANES = 128
XM, XP, YM, YP, CC, ZM, ZP, SM = (64 * i for i in range(8))
FACES = (XM, XP, YM, YP, ZM, ZP)


def split(v):
    hi = v.astype(BF16)
    lo = (v - hi.astype(F32)).astype(BF16)
    return jnp.concatenate([hi, lo, hi], axis=0)


def exact_dot(a, b):
    return jnp.dot(a, b, precision=lax.Precision.HIGHEST, preferred_element_type=F32)


def widen(w):
    hi = w.astype(BF16)
    lo = (w - hi.astype(F32)).astype(BF16)
    return jnp.concatenate([hi, hi, lo], axis=1)


def kernel(ngx, ngy, src_h, kap_h, diag_h, faces_h, smooth_h, prol_h, both_out,
           held, s_out, src, kap, diag, faces, smooth, prol, s_in, q0, u1, u2, u3, q1, u11, u21, e1, q2, u12, u22, e2, pp, pb, rr,
           wm, wl, wb, wr, wp,
           s_q0, r_q0, s_qx, r_qx, s_qc, r_qc, s_u2b, r_u2b, s_g, r_g, s_rl, r_rl, s_q2, r_q2, s_u21, r_u21):
    sol, res = held.at[0], held.at[1]

    def store(i):
        return pltpu.make_async_copy(held.at[i], both_out.at[pl.ds(N * 8 * i, N * 8)], s_out.at[i])

    gx, gy = lax.axis_index("gx"), lax.axis_index("gy")

    def inside(dx, dy):
        ok = None
        for at, d, n in ((gx, dx, ngx), (gy, dy, ngy)):
            if d:
                c = (at + d >= 0) & (at + d < n)
                ok = c if ok is None else ok & c
        return ok

    fetches = [pltpu.make_async_copy(a, b, s_in.at[i]) for i, (a, b) in enumerate((
        (src_h, src), (kap_h, kap), (smooth_h, smooth), (faces_h, faces), (diag_h, diag), (prol_h, prol)))]
    for f in fetches:
        f.start()

    barrier = pltpu.get_barrier_semaphore()
    partners = [(d, 0) for d in (-3, -2, -1, 1, 2, 3)] + [(0, d) for d in (-3, -2, -1, 1, 2, 3)]
    partners += [(a, b) for a in (-1, 1) for b in (-1, 1)]
    for dx, dy in partners:
        @pl.when(inside(dx, dy))
        def _():
            pl.semaphore_signal(barrier, inc=1, device_id=(gx + dx, gy + dy), device_id_type=MESH)
    fetches[1].wait()
    fetches[0].wait()
    for y in range(2):
        for x in range(4):
            c = x * 2 + y
            q0[2 + y, 2 + x] = src[pl.ds(c, N, stride=8), :] / kap[pl.ds(c, 1), :]
    peers = 0
    for dx, dy in partners:
        peers = peers + inside(dx, dy).astype(jnp.int32)
    pl.semaphore_wait(barrier, peers)

    def remote(s, d, ssem, rsem, dx, dy):
        return pltpu.make_async_remote_copy(
            src_ref=s, dst_ref=d, send_sem=ssem, recv_sem=rsem,
            device_id=(gx + dx, gy + dy), device_id_type=MESH)

    def send(s, d, ssem, rsem, dx, dy, cond=None):
        ok = inside(dx, dy) if cond is None else cond

        @pl.when(ok)
        def _():
            remote(s, d, ssem, rsem, dx, dy).start()

    def receive(d, ssem, rsem, dx, dy, cond=None):
        ok = inside(dx, dy) if cond is None else cond

        @pl.when(ok)
        def _():
            remote(d, d, ssem, rsem, dx, dy).wait_recv()

    def clear(ref, dx, dy):
        @pl.when(jnp.logical_not(inside(dx, dy)))
        def _():
            ref[...] = jnp.zeros(ref.shape, F32)

    def faces_x(buf):
        return [
            (buf.at[pl.ds(2, 2), 5], buf.at[pl.ds(2, 2), 1], 1, 0),
            (buf.at[pl.ds(2, 2), 2], buf.at[pl.ds(2, 2), 6], -1, 0),
            (buf.at[pl.ds(2, 2), 4], buf.at[pl.ds(2, 2), 0], 1, 0),
            (buf.at[pl.ds(2, 2), 3], buf.at[pl.ds(2, 2), 7], -1, 0),
        ]

    def near_y(buf, x, n):
        return [
            (buf.at[3, pl.ds(x, n)], buf.at[1, pl.ds(x, n)], 0, 1),
            (buf.at[2, pl.ds(x, n)], buf.at[4, pl.ds(x, n)], 0, -1),
        ]

    def far_y(buf, x, n):
        return [
            (buf.at[2, pl.ds(x, n)], buf.at[0, pl.ds(x, n)], 0, 1),
            (buf.at[3, pl.ds(x, n)], buf.at[5, pl.ds(x, n)], 0, -1),
        ]

    def corners(buf):
        return [
            (buf.at[3, 5], buf.at[1, 1], 1, 1),
            (buf.at[3, 2], buf.at[1, 6], -1, 1),
            (buf.at[2, 5], buf.at[4, 1], 1, -1),
            (buf.at[2, 2], buf.at[4, 6], -1, -1),
        ]

    def send_all(faces_of, ssem, rsem):
        for i, (s, d, dx, dy) in enumerate(faces_of):
            send(s, d, ssem.at[i], rsem.at[i], dx, dy)

    def receive_all(faces_of, ssem, rsem):
        for i, (s, d, dx, dy) in enumerate(faces_of):
            receive(d, ssem.at[i], rsem.at[i], -dx, -dy)

    q0_y = near_y(q0, 2, 1) + near_y(q0, 5, 1) + near_y(q0, 3, 2) + far_y(q0, 2, 2) + far_y(q0, 4, 2)
    q0_x = faces_x(q0)
    q0_c = [
        (q0.at[1, 5], q0.at[1, 1], 1, -1),
        (q0.at[4, 5], q0.at[4, 1], 1, 1),
        (q0.at[1, 2], q0.at[1, 6], -1, -1),
        (q0.at[4, 2], q0.at[4, 6], -1, 1),
    ]
    u2_more = far_y(u2, 2, 4) + faces_x(u2)[2:] + corners(u2)
    send_all(q0_y, s_q0, r_q0)
    send_all(q0_x, s_qx, r_qx)

    for f in fetches[2:]:
        f.wait()
    s8 = OMEGA * smooth[...]
    eye = (lax.broadcasted_iota(jnp.int32, (N, N), 0) == lax.broadcasted_iota(jnp.int32, (N, N), 1)).astype(F32)
    wm[pl.ds(SM, N), :] = widen(s8)
    for i, at in enumerate(FACES):
        f = faces[i]
        wb[pl.ds(at, N), :] = widen(-f)
        sf = exact_dot(s8, f)
        wl[pl.ds(at, N), :] = widen(sf)
        wm[pl.ds(at, N), :] = widen(exact_dot(sf, s8))
    d = diag[...]
    wb[pl.ds(CC, N), :] = widen(d)
    lc = eye - exact_dot(s8, d)
    wl[pl.ds(CC, N), :] = widen(lc)
    wm[pl.ds(CC, N), :] = widen(s8 + exact_dot(lc, s8))
    for i in range(4):
        p = prol[i]
        wp[pl.ds(N * i, N), :] = widen(p)
        wr[pl.ds(N * i, N), :] = widen(0.25 * p.T)

    for group in (q0_y, q0_x, u2_more):
        for _, dst, dx, dy in group:
            clear(dst, -dx, -dy)
    for _, dst, dx, dy in q0_c:
        clear(dst, -dx, dy)
    clear(q1.at[pl.ds(0, 2)], -1, 0)
    clear(q1.at[pl.ds(4, 2)], 1, 0)
    clear(u21.at[0], -1, 0)
    clear(u21.at[5], 1, 0)
    for dd in (1, 2, 3):
        clear(q2.at[3 - dd], -dd, 0)
        clear(q2.at[3 + dd], dd, 0)
    e1[:, 0] = jnp.zeros((4, N, LANES), F32)
    e1[:, 5] = jnp.zeros((4, N, LANES), F32)

    lane = lax.broadcasted_iota(jnp.int32, (N, LANES), 1)
    not_first, not_last = lane > 0, lane < LANES - 1

    def apply(w, row, rows, load, cols, at, to=pp):
        pair = jnp.concatenate([split(load(cols[0])), split(load(cols[1]))], axis=1)
        out = jnp.dot(w[pl.ds(row, rows), :], pair, preferred_element_type=F32)
        to[at[0], pl.ds(row, rows), :] = out[:, :LANES]
        to[at[1], pl.ds(row, rows), :] = out[:, LANES:]

    def gathered(c, sx, sy, ym=True, yp=True, of=pp):
        t = of[c, pl.ds(CC, N), :]
        t = t + of[c - sx, pl.ds(XM, N), :] + of[c + sx, pl.ds(XP, N), :]
        if ym:
            t = t + of[c - sy, pl.ds(YM, N), :]
        if yp:
            t = t + of[c + sy, pl.ds(YP, N), :]
        t = t + jnp.where(not_first, pltpu.roll(of[c, pl.ds(ZM, N), :], 1, 1), 0.0)
        t = t + jnp.where(not_last, pltpu.roll(of[c, pl.ds(ZP, N), :], LANES - 1, 1), 0.0)
        return t

    def loop(n, body):
        for i in range(n):
            body(i)

    def fine_at(y, x):
        return (y + 2) * 8 + x + 2

    def fine(w, row, rows, buf, c, e, to=pp):
        apply(w, row, rows, lambda p: buf[2 + p[0], 2 + p[1]], (c, e), (fine_at(*c), fine_at(*e)), to)

    def fine_own(w, rows, buf, to=pp):
        for y in range(2):
            for x in (0, 2):
                fine(w, 0, rows, buf, (y, x), (y, x + 1), to)

    def keep(ok):
        return jnp.where(ok, 1.0, 0.0).astype(F32)

    def present(offset):
        return keep((gx + offset >= 0) & (gx + offset < ngx))

    def side(offset):
        return keep((gy + offset >= 0) & (gy + offset < ngy))

    def take_u2(y, x, m=None):
        c = fine_at(y, x)
        v = gathered(c, 1, 8)
        u2[2 + y, 2 + x] = v if m is None else m * v
        u1[1 + y, 1 + x] = pp[c, pl.ds(SM, N), :]

    fine_own(wm, 512, q0)
    receive_all(q0_x, s_qx, r_qx)
    for y in range(2):
        fine(wm, 0, 512, q0, (y, -1), (y, 4))
        fine(wm, XM, 128, q0, (y, -2), (y, 5))

    def forward(group):
        for i, (s, d, dx, dy) in group:
            @pl.when(inside(dx, 0) & inside(0, dy))
            def _():
                pltpu.make_async_remote_copy(
                    src_ref=s, dst_ref=d, send_sem=s_qc.at[i], recv_sem=r_qc.at[i],
                    device_id=(gx + dx, gy), device_id_type=MESH).start()

    def receive_part(first, n):
        for i in range(first, first + n):
            s, d, dx, dy = q0_y[i]
            receive(d, s_q0.at[i], r_q0.at[i], -dx, -dy)

    receive_part(2, 2)
    forward([(0, q0_c[0]), (1, q0_c[1])])
    receive_part(0, 2)
    forward([(2, q0_c[2]), (3, q0_c[3])])
    receive_part(4, 2)
    for x in range(4):
        fine(wm, 0, 512, q0, (-1, x), (2, x))
    for y in range(2):
        for x in range(4):
            take_u2(y, x)
    fine_own(wb, 448, u2, pb)
    for i, (s, d, dx, dy) in enumerate(q0_c):
        @pl.when(inside(-dx, 0) & inside(0, dy))
        def _():
            pltpu.make_async_remote_copy(
                src_ref=d, dst_ref=d, send_sem=s_qc.at[i], recv_sem=r_qc.at[i],
                device_id=(gx - dx, gy), device_id_type=MESH).wait_recv()
    for y in (-1, 2):
        fine(wm, 0, 256, q0, (y, -1), (y, 4))
    for y in range(2):
        take_u2(y, -1, present(-1))
        take_u2(y, 4, present(1))
        fine(wb, XM, 128, u2, (y, -1), (y, 4), pb)

    def relay(j, at):
        for i, (dx, to) in enumerate(((1, 0), (-1, 4))):
            @pl.when(inside(dx, 0))
            def _():
                remote(q1.at[2 + at, j, pl.ds(0, N)], q1.at[to + at, j, pl.ds(0, N)], s_rl.at[i, at, j], r_rl.at[i, at, j], dx, 0).start()

    def half(at):
        receive_part(6 + 2 * at, 2)
        for x in (2 * at, 2 * at + 1):
            fine(wm, YM, 128, q0, (-2, x), (3, x))
        for x in (2 * at, 2 * at + 1):
            take_u2(-1, x, side(-1))
            take_u2(2, x, side(1))
        for x in (2 * at, 2 * at + 1):
            fine(wb, YM, 128, u2, (-1, x), (2, x), pb)
        total = None
        for x in (2 * at, 2 * at + 1):
            for y in range(2):
                t = gathered(fine_at(y, x), 1, 8, of=pb)
                k = kap[pl.ds(x * 2 + y, 1), :]
                r = split((q0[2 + y, 2 + x] - t) * k)
                child = 2 * (x - 2 * at) + y
                part = jnp.dot(wr[pl.ds(N * child, N), :], r, preferred_element_type=F32)
                total = part if total is None else total + part
        k1 = kap[pl.ds(4 * at, 1), :] + kap[pl.ds(4 * at + 1, 1), :]
        k1 = (k1 + (kap[pl.ds(4 * at + 2, 1), :] + kap[pl.ds(4 * at + 3, 1), :])) * 0.25
        q1[2 + at, gy, pl.ds(0, N), :] = total / k1
        q1[2 + at, gy, pl.ds(N, 8), :] = jnp.broadcast_to(k1, (8, LANES))
        for j in range(ngy):
            @pl.when(gy != j)
            def _():
                pltpu.make_async_remote_copy(
                    src_ref=q1.at[2 + at, gy], dst_ref=q1.at[2 + at, gy],
                    send_sem=s_g.at[at, j], recv_sem=r_g.at[at, gy],
                    device_id=(gx, j), device_id_type=MESH).start()
        relay(gy, at)

    half(0)
    half(1)

    def restrict(index):
        total = None
        for child in range(4):
            pair = jnp.concatenate([rr[index(0, child)], rr[index(1, child)]], axis=1)
            part = jnp.dot(wr[pl.ds(N * child, N), :], pair, preferred_element_type=F32)
            total = part if total is None else total + part
        return total[:, :LANES], total[:, LANES:]

    def arrive(j, at):
        block = q1.at[2 + at, j]
        pltpu.make_async_remote_copy(
            src_ref=block, dst_ref=block, send_sem=s_g.at[at, j], recv_sem=r_g.at[at, j],
            device_id=(gx, j), device_id_type=MESH).wait_recv()
        relay(j, at)
    for at in range(2):
        for dd in (1, -1, 2, -2, 3, -3):
            @pl.when(inside(0, dd))
            def _():
                arrive(gy + dd, at)
    send_all(u2_more, s_u2b, r_u2b)

    def coarse_own(w, rows, load, first, planes):
        def body(i):
            c = 4 * first + 2 * i
            apply(w, 0, rows, load, (c, c + 1), (c, c + 1))
        loop(2 * planes, body)

    def coarse_edges(w, load, low, high):
        def body(y):
            c, e = 4 * low + y, 4 * high + y
            apply(w, XM, 128, load, (c, e), (c, e))
        loop(4, body)

    def load_q1(c):
        return q1[c // 4, c % 4, pl.ds(0, N), :]

    def load_u21(c):
        return u21[c // 4, c % 4]

    coarse_own(wm, 512, load_q1, 2, 2)
    for at in range(2):
        for j in range(ngy):
            for i, (dx, to) in enumerate(((1, 0), (-1, 4))):
                @pl.when(inside(-dx, 0))
                def _():
                    block = q1.at[to + at, j, pl.ds(0, N)]
                    remote(block, block, s_rl.at[i, at, j], r_rl.at[i, at, j], -dx, 0).wait_recv()
        coarse_own(wm, 512, load_q1, 1 if at else 4, 1)
    coarse_edges(wm, load_q1, 0, 5)

    def device_of(x):
        return (x // 2) - 1

    def sum_u21(x):
        m = present(device_of(x))
        for y in range(4):
            c = 4 * x + y
            u21[x, y] = m * gathered(c, 4, 1, y > 0, y < 3)
            u11[x, y] = m * pp[c, pl.ds(SM, N), :]
    loop(4, lambda i: sum_u21(i + 1))

    low = pl.ds(jnp.clip(gy - 1, 0, ngy - 3), 3)
    u21_moves = [(u21.at[2, low], u21.at[0, low], 1, 0), (u21.at[3, low], u21.at[5, low], -1, 0)]
    send_all(u21_moves, s_u21, r_u21)
    coarse_own(wb, 448, load_u21, 2, 2)
    coarse_edges(wb, load_u21, 1, 4)

    def sum_r1(x):
        for y in range(4):
            t = gathered(4 * x + y, 4, 1, y > 0, y < 3)
            k1 = q1[x, y, pl.ds(N, 1), :]
            rr[(x - 2) * 4 + y] = split((q1[x, y, pl.ds(0, N), :] - t) * k1)
    loop(2, lambda i: sum_r1(i + 2))
    coarse2 = restrict(lambda at, child: (child // 2) * 4 + 2 * at + child % 2)
    for at in range(2):
        k2 = q1[2, 2 * at, pl.ds(N, 1), :] + q1[2, 2 * at + 1, pl.ds(N, 1), :]
        k2 = (k2 + (q1[3, 2 * at, pl.ds(N, 1), :] + q1[3, 2 * at + 1, pl.ds(N, 1), :])) * 0.25
        q2[3, at] = coarse2[at] / k2

    q2_moves = [(q2.at[3], q2.at[3 - dd], dd, 0) for dd in (3, -3, 2, -2, 1, -1)]
    send_all(q2_moves, s_q2, r_q2)

    def load_q2(c):
        return q2[c // 2, c % 2]

    def load_u22(c):
        return u22[c // 2, c % 2]

    def last_own(w, rows, load, first, planes):
        def body(i):
            c = 2 * first + 2 * i
            apply(w, 0, rows, load, (c, c + 1), (c, c + 1))
        loop(planes, body)

    def last_edges(w, load, low, high):
        def body(y):
            c, e = 2 * low + y, 2 * high + y
            apply(w, XM, 128, load, (c, e), (c, e))
        loop(2, body)

    last_own(wm, 512, load_q2, 3, 1)
    for group, ssem, rsem in ((q0_y, s_q0, r_q0), (q0_x, s_qx, r_qx)):
        for i, (s, dst, dx, dy) in enumerate(group):
            @pl.when(inside(dx, dy))
            def _():
                remote(s, dst, ssem.at[i], rsem.at[i], dx, dy).wait_send()
    for i, (s, d, dx, dy) in enumerate(q0_c):
        @pl.when(inside(dx, 0) & inside(0, dy))
        def _():
            pltpu.make_async_remote_copy(
                src_ref=s, dst_ref=d, send_sem=s_qc.at[i], recv_sem=r_qc.at[i],
                device_id=(gx + dx, gy), device_id_type=MESH).wait_send()
    for at in range(2):
        for j in range(ngy):
            block = q1.at[2 + at, j]

            @pl.when(gy != j)
            def _():
                pltpu.make_async_remote_copy(
                    src_ref=block, dst_ref=block, send_sem=s_g.at[at, j], recv_sem=r_g.at[at, j],
                    device_id=(gx, j), device_id_type=MESH).wait_send()
            for i, (dx, to) in enumerate(((1, 0), (-1, 4))):
                @pl.when(inside(dx, 0))
                def _():
                    remote(block.at[pl.ds(0, N)], q1.at[to + at, j, pl.ds(0, N)], s_rl.at[i, at, j], r_rl.at[i, at, j], dx, 0).wait_send()
    def receive_q2(distance):
        for i, (s, d, dx, dy) in enumerate(q2_moves):
            if abs(dx) == distance:
                receive(d, s_q2.at[i], r_q2.at[i], -dx, -dy)

    receive_q2(1)
    last_own(wm, 512, load_q2, 2, 1)
    last_own(wm, 512, load_q2, 4, 1)
    receive_q2(2)
    last_own(wm, 512, load_q2, 1, 1)
    last_own(wm, 512, load_q2, 5, 1)
    receive_q2(3)
    last_edges(wm, load_q2, 0, 6)

    def sum_u22(x):
        m = present(x - 3)
        for y in range(2):
            u22[x, y] = m * gathered(2 * x + y, 2, 1, y > 0, y < 1)
            u12[x, y] = pp[2 * x + y, pl.ds(SM, N), :]
    loop(5, lambda i: sum_u22(i + 1))
    last_own(wl, 448, load_u22, 2, 3)
    last_edges(wl, load_u22, 1, 5)

    def sum_e2(x):
        m = present(x - 3)
        for y in range(2):
            e2[x - 2, y] = m * (u12[x, y] + gathered(2 * x + y, 2, 1, y > 0, y < 1))
    loop(3, lambda i: sum_e2(i + 2))

    receive_all(u21_moves, s_u21, r_u21)

    def prolong(load):
        pair = jnp.concatenate([split(load(0)), split(load(1))], axis=1)
        out = jnp.dot(wp[...], pair, preferred_element_type=F32)
        return lambda at, child: out[N * child:N * (child + 1), LANES * at:LANES * (at + 1)]

    for i, (s, dst, dx, dy) in enumerate(q2_moves):
        @pl.when(inside(dx, dy))
        def _():
            remote(s, dst, s_q2.at[i], r_q2.at[i], dx, dy).wait_send()

    for i, (s, dst, dx, dy) in enumerate(u21_moves):
        @pl.when(inside(dx, dy))
        def _():
            remote(s, dst, s_u21.at[i], r_u21.at[i], dx, dy).wait_send()

    def lift1(x2):
        part = prolong(lambda y: e2[x2, y])
        for y2 in range(2):
            for child in range(4):
                x, y = 2 * x2 + child // 2, 2 * y2 + child % 2
                u21[x, y] = u21[x, y] + part(y2, child)
    loop(3, lift1)
    coarse_own(wl, 448, load_u21, 1, 4)
    coarse_edges(wl, load_u21, 0, 5)

    def sum_e1(x):
        m = present(device_of(x))
        for y in range(4):
            e1[x - 1, 1 + y] = m * (u11[x, y] + gathered(4 * x + y, 4, 1, y > 0, y < 3))
    loop(4, lambda i: sum_e1(i + 1))

    receive_all(u2_more, s_u2b, r_u2b)
    for i, (s, dst, dx, dy) in enumerate(u2_more):
        @pl.when(inside(dx, dy))
        def _():
            remote(s, dst, s_u2b.at[i], r_u2b.at[i], dx, dy).wait_send()

    wanted = {(y, x) for y in range(-2, 4) for x in range(-2, 6)
              if max(0, -y, y - 1) + max(0, -x, x - 3) <= 2}
    for j in range(3):
        for xp in range(2):
            part = prolong(lambda i: e1[2 * xp + i, gy + j])
            for i in range(2):
                for child in range(4):
                    x = 2 * (2 * xp + i - 1) + child // 2
                    y = 2 * (j - 1) + child % 2
                    if (y, x) in wanted:
                        u2[2 + y, 2 + x] = u2[2 + y, 2 + x] + part(i, child)

    def load_u2(c):
        return u2[2 + c[0], 2 + c[1]]

    def both(w, row, rows, c, e):
        apply(w, row, rows, load_u2, (c, e), (fine_at(*c), fine_at(*e)))

    def rows_wide(i):
        y, x = i // 3, (i % 3) * 2 - 1
        both(wl, 0, 448, (y, x), (y, x + 1))
    loop(6, rows_wide)

    def rows_short(i):
        y, x = (i // 2) * 3 - 1, (i % 2) * 2
        both(wl, 0, 448, (y, x), (y, x + 1))
    loop(4, rows_short)
    loop(2, lambda y: both(wl, XM, 128, (y, -2), (y, 5)))
    loop(4, lambda x: both(wl, YM, 128, (-2, x), (3, x)))
    loop(2, lambda i: both(wl, 0, 256, (3 * i - 1, -1), (3 * i - 1, 4)))

    def sum_u3(y, x, m=None):
        v = u1[1 + y, 1 + x] + gathered(fine_at(y, x), 1, 8)
        u3[2 + y, 2 + x] = v if m is None else m * v
        return v

    def own_u3(i):
        y, x = i // 4, i % 4
        v = sum_u3(y, x)
        sol[pl.ds(x * 2 + y, N, stride=8), :] = v
    loop(8, own_u3)
    store(0).start()
    loop(2, lambda y: sum_u3(y, -1, present(-1)))
    loop(2, lambda y: sum_u3(y, 4, present(1)))
    loop(4, lambda x: sum_u3(-1, x, keep(gy > 0)))
    loop(4, lambda x: sum_u3(2, x, keep(gy < ngy - 1)))
    fine_own(wb, 448, u3)
    for y in range(2):
        fine(wb, XM, 128, u3, (y, -1), (y, 4))
    for x in range(4):
        fine(wb, YM, 128, u3, (-1, x), (2, x))

    def final(i):
        y, x = i // 4, i % 4
        c = x * 2 + y
        t = gathered(fine_at(y, x), 1, 8)
        res[pl.ds(c, N, stride=8), :] = src[pl.ds(c, N, stride=8), :] - kap[pl.ds(c, 1), :] * t
    loop(8, final)
    store(1).start()

    store(0).wait()
    store(1).wait()


def solution(mesh):
    ngx, ngy = mesh.shape["gx"], mesh.shape["gy"]

    def shards(source, conductivity, diag_block, face_blocks, smoother, prolong):
        dma = pltpu.SemaphoreType.DMA
        col = (N, LANES)
        scratch = [
            pltpu.VMEM((2, N * 8, LANES), F32),
            dma((2,)),
            pltpu.VMEM((N * 8, LANES), F32),
            pltpu.VMEM((8, LANES), F32),
            pltpu.VMEM((N, N), F32),
            pltpu.VMEM((6, N, N), F32),
            pltpu.VMEM((N, N), F32),
            pltpu.VMEM((4, N, N), F32),
            dma((6,)),
            pltpu.VMEM((6, 8) + col, F32),
            pltpu.VMEM((4, 6) + col, F32),
            pltpu.VMEM((6, 8) + col, F32),
            pltpu.VMEM((6, 8) + col, F32),
            pltpu.VMEM((6, 4, N + 8, LANES), F32),
            pltpu.VMEM((6, 4) + col, F32),
            pltpu.VMEM((6, 4) + col, F32),
            pltpu.VMEM((4, 6) + col, F32),
            pltpu.VMEM((7, 2) + col, F32),
            pltpu.VMEM((7, 2) + col, F32),
            pltpu.VMEM((7, 2) + col, F32),
            pltpu.VMEM((3, 2) + col, F32),
            pltpu.VMEM((48, 512, LANES), F32),
            pltpu.VMEM((48, 448, LANES), F32),
            pltpu.VMEM((8, 192, LANES), BF16),
            pltpu.VMEM((512, 192), BF16),
            pltpu.VMEM((448, 192), BF16),
            pltpu.VMEM((448, 192), BF16),
            pltpu.VMEM((256, 192), BF16),
            pltpu.VMEM((256, 192), BF16),
            dma((10,)), dma((10,)), dma((4,)), dma((4,)), dma((4,)), dma((4,)), dma((8,)), dma((8,)),
            dma((2, 4)), dma((2, 4)), dma((2, 2, 4)), dma((2, 2, 4)), dma((6,)), dma((6,)), dma((2,)), dma((2,)),
        ]
        shape = source.shape
        flat = jax.ShapeDtypeStruct((2 * N * 8, LANES), F32)
        both = pl.pallas_call(
            functools.partial(kernel, ngx, ngy),
            out_shape=flat,
            in_specs=[pl.BlockSpec(memory_space=pl.ANY)] * 6,
            out_specs=pl.BlockSpec(memory_space=pl.ANY),
            scratch_shapes=scratch,
            compiler_params=pltpu.CompilerParams(
                collective_id=0, has_side_effects=True, vmem_limit_bytes=60 << 20),
            cost_estimate=pl.CostEstimate(flops=10**9, bytes_accessed=10**6, transcendentals=0),
        )(source.reshape(N * 8, LANES), conductivity.reshape(8, LANES),
          diag_block, face_blocks, smoother, prolong)
        return both[:N * 8].reshape(shape), both[N * 8:].reshape(shape)

    return jax.shard_map(
        shards,
        mesh=mesh,
        in_specs=(P(None, "gx", "gy", None), P("gx", "gy", None), P(), P(), P(), P()),
        out_specs=(P(None, "gx", "gy", None), P(None, "gx", "gy", None)),
        check_vma=False,
    )
```

```python
import functools

import jax
import jax.numpy as jnp
from jax import lax
from jax.experimental import pallas as pl
from jax.experimental.pallas import tpu as pltpu
from jax.sharding import PartitionSpec as P

MESH = pl.DeviceIdType.MESH
F32 = jnp.float32
BF16 = jnp.bfloat16
OMEGA = 0.8
N = 64
LANES = 128
XM, XP, YM, YP, CC, ZM, ZP, SM = (64 * i for i in range(8))
FACES = (XM, XP, YM, YP, ZM, ZP)


def split(v):
    hi = v.astype(BF16)
    lo = (v - hi.astype(F32)).astype(BF16)
    return jnp.concatenate([hi, lo, hi], axis=0)


def exact_dot(a, b):
    return jnp.dot(a, b, precision=lax.Precision.HIGHEST, preferred_element_type=F32)


def widen(w):
    hi = w.astype(BF16)
    lo = (w - hi.astype(F32)).astype(BF16)
    return jnp.concatenate([hi, hi, lo], axis=1)


def kernel(ngx, ngy, src_h, kap_h, diag_h, faces_h, smooth_h, prol_h, both_out,
           held, s_out, src, kap, diag, faces, smooth, prol, s_in, q0, u1, u2, u3, q1, u11, u21, e1, q2, u12, u22, e2, pp, pb, rr,
           wm, wl, wb, wr, wp,
           s_q0, r_q0, s_qx, r_qx, s_qc, r_qc, s_u2b, r_u2b, s_g, r_g, s_rl, r_rl, s_q2, r_q2, s_u21, r_u21):
    sol, res = held.at[0], held.at[1]

    def store(i):
        return pltpu.make_async_copy(held.at[i], both_out.at[pl.ds(N * 8 * i, N * 8)], s_out.at[i])

    gx, gy = lax.axis_index("gx"), lax.axis_index("gy")

    def inside(dx, dy):
        ok = None
        for at, d, n in ((gx, dx, ngx), (gy, dy, ngy)):
            if d:
                c = (at + d >= 0) & (at + d < n)
                ok = c if ok is None else ok & c
        return ok

    fetches = [pltpu.make_async_copy(a, b, s_in.at[i]) for i, (a, b) in enumerate((
        (src_h, src), (kap_h, kap), (smooth_h, smooth), (faces_h, faces), (diag_h, diag), (prol_h, prol)))]
    for f in fetches:
        f.start()

    barrier = pltpu.get_barrier_semaphore()
    partners = [(d, 0) for d in (-3, -2, -1, 1, 2, 3)] + [(0, d) for d in (-3, -2, -1, 1, 2, 3)]
    partners += [(a, b) for a in (-1, 1) for b in (-1, 1)]
    for dx, dy in partners:
        @pl.when(inside(dx, dy))
        def _():
            pl.semaphore_signal(barrier, inc=1, device_id=(gx + dx, gy + dy), device_id_type=MESH)
    fetches[1].wait()
    fetches[0].wait()
    for y in range(2):
        for x in range(4):
            c = x * 2 + y
            q0[2 + y, 2 + x] = src[pl.ds(c, N, stride=8), :] / kap[pl.ds(c, 1), :]
    peers = 0
    for dx, dy in partners:
        peers = peers + inside(dx, dy).astype(jnp.int32)
    pl.semaphore_wait(barrier, peers)

    def remote(s, d, ssem, rsem, dx, dy):
        return pltpu.make_async_remote_copy(
            src_ref=s, dst_ref=d, send_sem=ssem, recv_sem=rsem,
            device_id=(gx + dx, gy + dy), device_id_type=MESH)

    def send(s, d, ssem, rsem, dx, dy, cond=None):
        ok = inside(dx, dy) if cond is None else cond

        @pl.when(ok)
        def _():
            remote(s, d, ssem, rsem, dx, dy).start()

    def receive(d, ssem, rsem, dx, dy, cond=None):
        ok = inside(dx, dy) if cond is None else cond

        @pl.when(ok)
        def _():
            remote(d, d, ssem, rsem, dx, dy).wait_recv()

    def clear(ref, dx, dy):
        @pl.when(jnp.logical_not(inside(dx, dy)))
        def _():
            ref[...] = jnp.zeros(ref.shape, F32)

    def faces_x(buf):
        return [
            (buf.at[pl.ds(2, 2), 5], buf.at[pl.ds(2, 2), 1], 1, 0),
            (buf.at[pl.ds(2, 2), 2], buf.at[pl.ds(2, 2), 6], -1, 0),
            (buf.at[pl.ds(2, 2), 4], buf.at[pl.ds(2, 2), 0], 1, 0),
            (buf.at[pl.ds(2, 2), 3], buf.at[pl.ds(2, 2), 7], -1, 0),
        ]

    def near_y(buf, x, n):
        return [
            (buf.at[3, pl.ds(x, n)], buf.at[1, pl.ds(x, n)], 0, 1),
            (buf.at[2, pl.ds(x, n)], buf.at[4, pl.ds(x, n)], 0, -1),
        ]

    def far_y(buf, x, n):
        return [
            (buf.at[2, pl.ds(x, n)], buf.at[0, pl.ds(x, n)], 0, 1),
            (buf.at[3, pl.ds(x, n)], buf.at[5, pl.ds(x, n)], 0, -1),
        ]

    def corners(buf):
        return [
            (buf.at[3, 5], buf.at[1, 1], 1, 1),
            (buf.at[3, 2], buf.at[1, 6], -1, 1),
            (buf.at[2, 5], buf.at[4, 1], 1, -1),
            (buf.at[2, 2], buf.at[4, 6], -1, -1),
        ]

    def send_all(faces_of, ssem, rsem):
        for i, (s, d, dx, dy) in enumerate(faces_of):
            send(s, d, ssem.at[i], rsem.at[i], dx, dy)

    def receive_all(faces_of, ssem, rsem):
        for i, (s, d, dx, dy) in enumerate(faces_of):
            receive(d, ssem.at[i], rsem.at[i], -dx, -dy)

    q0_y = near_y(q0, 2, 1) + near_y(q0, 5, 1) + near_y(q0, 3, 2) + far_y(q0, 2, 2) + far_y(q0, 4, 2)
    q0_x = faces_x(q0)
    q0_c = [
        (q0.at[1, 5], q0.at[1, 1], 1, -1),
        (q0.at[4, 5], q0.at[4, 1], 1, 1),
        (q0.at[1, 2], q0.at[1, 6], -1, -1),
        (q0.at[4, 2], q0.at[4, 6], -1, 1),
    ]
    u2_more = far_y(u2, 2, 4) + faces_x(u2)[2:] + corners(u2)
    send_all(q0_y, s_q0, r_q0)
    send_all(q0_x, s_qx, r_qx)

    for f in fetches[2:]:
        f.wait()
    s8 = OMEGA * smooth[...]
    eye = (lax.broadcasted_iota(jnp.int32, (N, N), 0) == lax.broadcasted_iota(jnp.int32, (N, N), 1)).astype(F32)
    wm[pl.ds(SM, N), :] = widen(s8)
    for i, at in enumerate(FACES):
        f = faces[i]
        wb[pl.ds(at, N), :] = widen(-f)
        sf = exact_dot(s8, f)
        wl[pl.ds(at, N), :] = widen(sf)
        wm[pl.ds(at, N), :] = widen(exact_dot(sf, s8))
    d = diag[...]
    wb[pl.ds(CC, N), :] = widen(d)
    lc = eye - exact_dot(s8, d)
    wl[pl.ds(CC, N), :] = widen(lc)
    wm[pl.ds(CC, N), :] = widen(s8 + exact_dot(lc, s8))
    for i in range(4):
        p = prol[i]
        wp[pl.ds(N * i, N), :] = widen(p)
        wr[pl.ds(N * i, N), :] = widen(0.25 * p.T)

    for group in (q0_y, q0_x, u2_more):
        for _, dst, dx, dy in group:
            clear(dst, -dx, -dy)
    for _, dst, dx, dy in q0_c:
        clear(dst, -dx, dy)
    clear(q1.at[pl.ds(0, 2)], -1, 0)
    clear(q1.at[pl.ds(4, 2)], 1, 0)
    clear(u21.at[0], -1, 0)
    clear(u21.at[5], 1, 0)
    for dd in (1, 2, 3):
        clear(q2.at[3 - dd], -dd, 0)
        clear(q2.at[3 + dd], dd, 0)
    e1[:, 0] = jnp.zeros((4, N, LANES), F32)
    e1[:, 5] = jnp.zeros((4, N, LANES), F32)

    lane = lax.broadcasted_iota(jnp.int32, (N, LANES), 1)
    not_first, not_last = lane > 0, lane < LANES - 1

    def apply(w, row, rows, load, cols, at, to=pp):
        pair = jnp.concatenate([split(load(cols[0])), split(load(cols[1]))], axis=1)
        out = jnp.dot(w[pl.ds(row, rows), :], pair, preferred_element_type=F32)
        to[at[0], pl.ds(row, rows), :] = out[:, :LANES]
        to[at[1], pl.ds(row, rows), :] = out[:, LANES:]

    def gathered(c, sx, sy, ym=True, yp=True, of=pp):
        t = of[c, pl.ds(CC, N), :]
        t = t + of[c - sx, pl.ds(XM, N), :] + of[c + sx, pl.ds(XP, N), :]
        if ym:
            t = t + of[c - sy, pl.ds(YM, N), :]
        if yp:
            t = t + of[c + sy, pl.ds(YP, N), :]
        t = t + jnp.where(not_first, pltpu.roll(of[c, pl.ds(ZM, N), :], 1, 1), 0.0)
        t = t + jnp.where(not_last, pltpu.roll(of[c, pl.ds(ZP, N), :], LANES - 1, 1), 0.0)
        return t

    def loop(n, body):
        for i in range(n):
            body(i)

    def fine_at(y, x):
        return (y + 2) * 8 + x + 2

    def fine(w, row, rows, buf, c, e, to=pp):
        apply(w, row, rows, lambda p: buf[2 + p[0], 2 + p[1]], (c, e), (fine_at(*c), fine_at(*e)), to)

    def fine_own(w, rows, buf, to=pp):
        for y in range(2):
            for x in (0, 2):
                fine(w, 0, rows, buf, (y, x), (y, x + 1), to)

    def keep(ok):
        return jnp.where(ok, 1.0, 0.0).astype(F32)

    def present(offset):
        return keep((gx + offset >= 0) & (gx + offset < ngx))

    def side(offset):
        return keep((gy + offset >= 0) & (gy + offset < ngy))

    def take_u2(y, x, m=None):
        c = fine_at(y, x)
        v = gathered(c, 1, 8)
        u2[2 + y, 2 + x] = v if m is None else m * v
        u1[1 + y, 1 + x] = pp[c, pl.ds(SM, N), :]

    fine_own(wm, 512, q0)
    receive_all(q0_x, s_qx, r_qx)
    for y in range(2):
        fine(wm, 0, 512, q0, (y, -1), (y, 4))
        fine(wm, XM, 128, q0, (y, -2), (y, 5))

    def forward(group):
        for i, (s, d, dx, dy) in group:
            @pl.when(inside(dx, 0) & inside(0, dy))
            def _():
                pltpu.make_async_remote_copy(
                    src_ref=s, dst_ref=d, send_sem=s_qc.at[i], recv_sem=r_qc.at[i],
                    device_id=(gx + dx, gy), device_id_type=MESH).start()

    def receive_part(first, n):
        for i in range(first, first + n):
            s, d, dx, dy = q0_y[i]
            receive(d, s_q0.at[i], r_q0.at[i], -dx, -dy)

    receive_part(2, 2)
    forward([(0, q0_c[0]), (1, q0_c[1])])
    receive_part(0, 2)
    forward([(2, q0_c[2]), (3, q0_c[3])])
    receive_part(4, 2)
    for x in range(4):
        fine(wm, 0, 512, q0, (-1, x), (2, x))
    for y in range(2):
        for x in range(4):
            take_u2(y, x)
    fine_own(wb, 448, u2, pb)
    for i, (s, d, dx, dy) in enumerate(q0_c):
        @pl.when(inside(-dx, 0) & inside(0, dy))
        def _():
            pltpu.make_async_remote_copy(
                src_ref=d, dst_ref=d, send_sem=s_qc.at[i], recv_sem=r_qc.at[i],
                device_id=(gx - dx, gy), device_id_type=MESH).wait_recv()
    for y in (-1, 2):
        fine(wm, 0, 256, q0, (y, -1), (y, 4))
    for y in range(2):
        take_u2(y, -1, present(-1))
        take_u2(y, 4, present(1))
        fine(wb, XM, 128, u2, (y, -1), (y, 4), pb)

    def relay(j, at):
        for i, (dx, to) in enumerate(((1, 0), (-1, 4))):
            @pl.when(inside(dx, 0))
            def _():
                remote(q1.at[2 + at, j, pl.ds(0, N)], q1.at[to + at, j, pl.ds(0, N)], s_rl.at[i, at, j], r_rl.at[i, at, j], dx, 0).start()

    def half(at):
        receive_part(6 + 2 * at, 2)
        for x in (2 * at, 2 * at + 1):
            fine(wm, YM, 128, q0, (-2, x), (3, x))
        for x in (2 * at, 2 * at + 1):
            take_u2(-1, x, side(-1))
            take_u2(2, x, side(1))
        for x in (2 * at, 2 * at + 1):
            fine(wb, YM, 128, u2, (-1, x), (2, x), pb)
        total = None
        for x in (2 * at, 2 * at + 1):
            for y in range(2):
                t = gathered(fine_at(y, x), 1, 8, of=pb)
                k = kap[pl.ds(x * 2 + y, 1), :]
                r = split((q0[2 + y, 2 + x] - t) * k)
                child = 2 * (x - 2 * at) + y
                part = jnp.dot(wr[pl.ds(N * child, N), :], r, preferred_element_type=F32)
                total = part if total is None else total + part
        k1 = kap[pl.ds(4 * at, 1), :] + kap[pl.ds(4 * at + 1, 1), :]
        k1 = (k1 + (kap[pl.ds(4 * at + 2, 1), :] + kap[pl.ds(4 * at + 3, 1), :])) * 0.25
        q1[2 + at, gy, pl.ds(0, N), :] = total / k1
        q1[2 + at, gy, pl.ds(N, 8), :] = jnp.broadcast_to(k1, (8, LANES))
        for j in range(ngy):
            @pl.when(gy != j)
            def _():
                pltpu.make_async_remote_copy(
                    src_ref=q1.at[2 + at, gy], dst_ref=q1.at[2 + at, gy],
                    send_sem=s_g.at[at, j], recv_sem=r_g.at[at, gy],
                    device_id=(gx, j), device_id_type=MESH).start()
        relay(gy, at)

    half(0)
    half(1)

    def restrict(index):
        total = None
        for child in range(4):
            pair = jnp.concatenate([rr[index(0, child)], rr[index(1, child)]], axis=1)
            part = jnp.dot(wr[pl.ds(N * child, N), :], pair, preferred_element_type=F32)
            total = part if total is None else total + part
        return total[:, :LANES], total[:, LANES:]

    def arrive(j, at):
        block = q1.at[2 + at, j]
        pltpu.make_async_remote_copy(
            src_ref=block, dst_ref=block, send_sem=s_g.at[at, j], recv_sem=r_g.at[at, j],
            device_id=(gx, j), device_id_type=MESH).wait_recv()
        relay(j, at)
    for at in range(2):
        for dd in (1, -1, 2, -2, 3, -3):
            @pl.when(inside(0, dd))
            def _():
                arrive(gy + dd, at)
    send_all(u2_more, s_u2b, r_u2b)

    def coarse_own(w, rows, load, first, planes):
        def body(i):
            c = 4 * first + 2 * i
            apply(w, 0, rows, load, (c, c + 1), (c, c + 1))
        loop(2 * planes, body)

    def coarse_edges(w, load, low, high):
        def body(y):
            c, e = 4 * low + y, 4 * high + y
            apply(w, XM, 128, load, (c, e), (c, e))
        loop(4, body)

    def load_q1(c):
        return q1[c // 4, c % 4, pl.ds(0, N), :]

    def load_u21(c):
        return u21[c // 4, c % 4]

    coarse_own(wm, 512, load_q1, 2, 2)
    for at in range(2):
        for j in range(ngy):
            for i, (dx, to) in enumerate(((1, 0), (-1, 4))):
                @pl.when(inside(-dx, 0))
                def _():
                    block = q1.at[to + at, j, pl.ds(0, N)]
                    remote(block, block, s_rl.at[i, at, j], r_rl.at[i, at, j], -dx, 0).wait_recv()
        coarse_own(wm, 512, load_q1, 1 if at else 4, 1)
    coarse_edges(wm, load_q1, 0, 5)

    def device_of(x):
        return (x // 2) - 1

    def sum_u21(x):
        m = present(device_of(x))
        for y in range(4):
            c = 4 * x + y
            u21[x, y] = m * gathered(c, 4, 1, y > 0, y < 3)
            u11[x, y] = m * pp[c, pl.ds(SM, N), :]
    loop(4, lambda i: sum_u21(i + 1))

    low = pl.ds(jnp.clip(gy - 1, 0, ngy - 3), 3)
    u21_moves = [(u21.at[2, low], u21.at[0, low], 1, 0), (u21.at[3, low], u21.at[5, low], -1, 0)]
    coarse_own(wb, 448, load_u21, 2, 2)
    coarse_edges(wb, load_u21, 1, 4)

    def sum_r1(x):
        for y in range(4):
            t = gathered(4 * x + y, 4, 1, y > 0, y < 3)
            k1 = q1[x, y, pl.ds(N, 1), :]
            rr[(x - 2) * 4 + y] = split((q1[x, y, pl.ds(0, N), :] - t) * k1)
    loop(2, lambda i: sum_r1(i + 2))
    coarse2 = restrict(lambda at, child: (child // 2) * 4 + 2 * at + child % 2)
    for at in range(2):
        k2 = q1[2, 2 * at, pl.ds(N, 1), :] + q1[2, 2 * at + 1, pl.ds(N, 1), :]
        k2 = (k2 + (q1[3, 2 * at, pl.ds(N, 1), :] + q1[3, 2 * at + 1, pl.ds(N, 1), :])) * 0.25
        q2[3, at] = coarse2[at] / k2

    q2_moves = [(q2.at[3], q2.at[3 - dd], dd, 0) for dd in (3, -3, 2, -2, 1, -1)]
    send_all(q2_moves, s_q2, r_q2)
    send_all(u21_moves, s_u21, r_u21)

    def load_q2(c):
        return q2[c // 2, c % 2]

    def load_u22(c):
        return u22[c // 2, c % 2]

    def last_own(w, rows, load, first, planes):
        def body(i):
            c = 2 * first + 2 * i
            apply(w, 0, rows, load, (c, c + 1), (c, c + 1))
        loop(planes, body)

    def last_edges(w, load, low, high):
        def body(y):
            c, e = 2 * low + y, 2 * high + y
            apply(w, XM, 128, load, (c, e), (c, e))
        loop(2, body)

    last_own(wm, 512, load_q2, 3, 1)
    for group, ssem, rsem in ((q0_y, s_q0, r_q0), (q0_x, s_qx, r_qx)):
        for i, (s, dst, dx, dy) in enumerate(group):
            @pl.when(inside(dx, dy))
            def _():
                remote(s, dst, ssem.at[i], rsem.at[i], dx, dy).wait_send()
    for i, (s, d, dx, dy) in enumerate(q0_c):
        @pl.when(inside(dx, 0) & inside(0, dy))
        def _():
            pltpu.make_async_remote_copy(
                src_ref=s, dst_ref=d, send_sem=s_qc.at[i], recv_sem=r_qc.at[i],
                device_id=(gx + dx, gy), device_id_type=MESH).wait_send()
    for at in range(2):
        for j in range(ngy):
            block = q1.at[2 + at, j]

            @pl.when(gy != j)
            def _():
                pltpu.make_async_remote_copy(
                    src_ref=block, dst_ref=block, send_sem=s_g.at[at, j], recv_sem=r_g.at[at, j],
                    device_id=(gx, j), device_id_type=MESH).wait_send()
            for i, (dx, to) in enumerate(((1, 0), (-1, 4))):
                @pl.when(inside(dx, 0))
                def _():
                    remote(block.at[pl.ds(0, N)], q1.at[to + at, j, pl.ds(0, N)], s_rl.at[i, at, j], r_rl.at[i, at, j], dx, 0).wait_send()
    def receive_q2(distance):
        for i, (s, d, dx, dy) in enumerate(q2_moves):
            if abs(dx) == distance:
                receive(d, s_q2.at[i], r_q2.at[i], -dx, -dy)

    receive_q2(1)
    last_own(wm, 512, load_q2, 2, 1)
    last_own(wm, 512, load_q2, 4, 1)
    receive_q2(2)
    last_own(wm, 512, load_q2, 1, 1)
    last_own(wm, 512, load_q2, 5, 1)
    receive_q2(3)
    last_edges(wm, load_q2, 0, 6)

    def sum_u22(x):
        m = present(x - 3)
        for y in range(2):
            u22[x, y] = m * gathered(2 * x + y, 2, 1, y > 0, y < 1)
            u12[x, y] = pp[2 * x + y, pl.ds(SM, N), :]
    loop(5, lambda i: sum_u22(i + 1))
    last_own(wl, 448, load_u22, 2, 3)
    last_edges(wl, load_u22, 1, 5)

    def sum_e2(x):
        m = present(x - 3)
        for y in range(2):
            e2[x - 2, y] = m * (u12[x, y] + gathered(2 * x + y, 2, 1, y > 0, y < 1))
    loop(3, lambda i: sum_e2(i + 2))

    receive_all(u21_moves, s_u21, r_u21)

    def prolong(load):
        pair = jnp.concatenate([split(load(0)), split(load(1))], axis=1)
        out = jnp.dot(wp[...], pair, preferred_element_type=F32)
        return lambda at, child: out[N * child:N * (child + 1), LANES * at:LANES * (at + 1)]

    for i, (s, dst, dx, dy) in enumerate(q2_moves):
        @pl.when(inside(dx, dy))
        def _():
            remote(s, dst, s_q2.at[i], r_q2.at[i], dx, dy).wait_send()

    for i, (s, dst, dx, dy) in enumerate(u21_moves):
        @pl.when(inside(dx, dy))
        def _():
            remote(s, dst, s_u21.at[i], r_u21.at[i], dx, dy).wait_send()

    def lift1(x2):
        part = prolong(lambda y: e2[x2, y])
        for y2 in range(2):
            for child in range(4):
                x, y = 2 * x2 + child // 2, 2 * y2 + child % 2
                u21[x, y] = u21[x, y] + part(y2, child)
    loop(3, lift1)
    coarse_own(wl, 448, load_u21, 1, 4)
    coarse_edges(wl, load_u21, 0, 5)

    def sum_e1(x):
        m = present(device_of(x))
        for y in range(4):
            e1[x - 1, 1 + y] = m * (u11[x, y] + gathered(4 * x + y, 4, 1, y > 0, y < 3))
    loop(4, lambda i: sum_e1(i + 1))

    receive_all(u2_more, s_u2b, r_u2b)
    for i, (s, dst, dx, dy) in enumerate(u2_more):
        @pl.when(inside(dx, dy))
        def _():
            remote(s, dst, s_u2b.at[i], r_u2b.at[i], dx, dy).wait_send()

    wanted = {(y, x) for y in range(-2, 4) for x in range(-2, 6)
              if max(0, -y, y - 1) + max(0, -x, x - 3) <= 2}
    for j in range(3):
        for xp in range(2):
            part = prolong(lambda i: e1[2 * xp + i, gy + j])
            for i in range(2):
                for child in range(4):
                    x = 2 * (2 * xp + i - 1) + child // 2
                    y = 2 * (j - 1) + child % 2
                    if (y, x) in wanted:
                        u2[2 + y, 2 + x] = u2[2 + y, 2 + x] + part(i, child)

    def load_u2(c):
        return u2[2 + c[0], 2 + c[1]]

    def both(w, row, rows, c, e):
        apply(w, row, rows, load_u2, (c, e), (fine_at(*c), fine_at(*e)))

    def rows_wide(i):
        y, x = i // 3, (i % 3) * 2 - 1
        both(wl, 0, 448, (y, x), (y, x + 1))
    loop(6, rows_wide)

    def rows_short(i):
        y, x = (i // 2) * 3 - 1, (i % 2) * 2
        both(wl, 0, 448, (y, x), (y, x + 1))
    loop(4, rows_short)
    loop(2, lambda y: both(wl, XM, 128, (y, -2), (y, 5)))
    loop(4, lambda x: both(wl, YM, 128, (-2, x), (3, x)))
    loop(2, lambda i: both(wl, 0, 256, (3 * i - 1, -1), (3 * i - 1, 4)))

    def sum_u3(y, x, m=None):
        v = u1[1 + y, 1 + x] + gathered(fine_at(y, x), 1, 8)
        u3[2 + y, 2 + x] = v if m is None else m * v
        return v

    def own_u3(i):
        y, x = i // 4, i % 4
        v = sum_u3(y, x)
        sol[pl.ds(x * 2 + y, N, stride=8), :] = v
    loop(8, own_u3)
    store(0).start()
    loop(2, lambda y: sum_u3(y, -1, present(-1)))
    loop(2, lambda y: sum_u3(y, 4, present(1)))
    loop(4, lambda x: sum_u3(-1, x, keep(gy > 0)))
    loop(4, lambda x: sum_u3(2, x, keep(gy < ngy - 1)))
    fine_own(wb, 448, u3)
    for y in range(2):
        fine(wb, XM, 128, u3, (y, -1), (y, 4))
    for x in range(4):
        fine(wb, YM, 128, u3, (-1, x), (2, x))

    def final(i):
        y, x = i // 4, i % 4
        c = x * 2 + y
        t = gathered(fine_at(y, x), 1, 8)
        res[pl.ds(c, N, stride=8), :] = src[pl.ds(c, N, stride=8), :] - kap[pl.ds(c, 1), :] * t
    loop(8, final)
    store(1).start()

    store(0).wait()
    store(1).wait()


def solution(mesh):
    ngx, ngy = mesh.shape["gx"], mesh.shape["gy"]

    def shards(source, conductivity, diag_block, face_blocks, smoother, prolong):
        dma = pltpu.SemaphoreType.DMA
        col = (N, LANES)
        scratch = [
            pltpu.VMEM((2, N * 8, LANES), F32),
            dma((2,)),
            pltpu.VMEM((N * 8, LANES), F32),
            pltpu.VMEM((8, LANES), F32),
            pltpu.VMEM((N, N), F32),
            pltpu.VMEM((6, N, N), F32),
            pltpu.VMEM((N, N), F32),
            pltpu.VMEM((4, N, N), F32),
            dma((6,)),
            pltpu.VMEM((6, 8) + col, F32),
            pltpu.VMEM((4, 6) + col, F32),
            pltpu.VMEM((6, 8) + col, F32),
            pltpu.VMEM((6, 8) + col, F32),
            pltpu.VMEM((6, 4, N + 8, LANES), F32),
            pltpu.VMEM((6, 4) + col, F32),
            pltpu.VMEM((6, 4) + col, F32),
            pltpu.VMEM((4, 6) + col, F32),
            pltpu.VMEM((7, 2) + col, F32),
            pltpu.VMEM((7, 2) + col, F32),
            pltpu.VMEM((7, 2) + col, F32),
            pltpu.VMEM((3, 2) + col, F32),
            pltpu.VMEM((48, 512, LANES), F32),
            pltpu.VMEM((48, 448, LANES), F32),
            pltpu.VMEM((8, 192, LANES), BF16),
            pltpu.VMEM((512, 192), BF16),
            pltpu.VMEM((448, 192), BF16),
            pltpu.VMEM((448, 192), BF16),
            pltpu.VMEM((256, 192), BF16),
            pltpu.VMEM((256, 192), BF16),
            dma((10,)), dma((10,)), dma((4,)), dma((4,)), dma((4,)), dma((4,)), dma((8,)), dma((8,)),
            dma((2, 4)), dma((2, 4)), dma((2, 2, 4)), dma((2, 2, 4)), dma((6,)), dma((6,)), dma((2,)), dma((2,)),
        ]
        shape = source.shape
        flat = jax.ShapeDtypeStruct((2 * N * 8, LANES), F32)
        both = pl.pallas_call(
            functools.partial(kernel, ngx, ngy),
            out_shape=flat,
            in_specs=[pl.BlockSpec(memory_space=pl.ANY)] * 6,
            out_specs=pl.BlockSpec(memory_space=pl.ANY),
            scratch_shapes=scratch,
            compiler_params=pltpu.CompilerParams(
                collective_id=0, has_side_effects=True, vmem_limit_bytes=60 << 20),
            cost_estimate=pl.CostEstimate(flops=10**9, bytes_accessed=10**6, transcendentals=0),
        )(source.reshape(N * 8, LANES), conductivity.reshape(8, LANES),
          diag_block, face_blocks, smoother, prolong)
        return both[:N * 8].reshape(shape), both[N * 8:].reshape(shape)

    return jax.shard_map(
        shards,
        mesh=mesh,
        in_specs=(P(None, "gx", "gy", None), P("gx", "gy", None), P(), P(), P(), P()),
        out_specs=(P(None, "gx", "gy", None), P(None, "gx", "gy", None)),
        check_vma=False,
    )
```

```python
import functools

import jax
import jax.numpy as jnp
from jax import lax
from jax.experimental import pallas as pl
from jax.experimental.pallas import tpu as pltpu
from jax.sharding import PartitionSpec as P

MESH = pl.DeviceIdType.MESH
F32 = jnp.float32
BF16 = jnp.bfloat16
OMEGA = 0.8
N = 64
LANES = 128
XM, XP, YM, YP, CC, ZM, ZP, SM = (64 * i for i in range(8))
FACES = (XM, XP, YM, YP, ZM, ZP)


def split(v):
    hi = v.astype(BF16)
    lo = (v - hi.astype(F32)).astype(BF16)
    return jnp.concatenate([hi, lo, hi], axis=0)


def exact_dot(a, b):
    return jnp.dot(a, b, precision=lax.Precision.HIGHEST, preferred_element_type=F32)


def widen(w):
    hi = w.astype(BF16)
    lo = (w - hi.astype(F32)).astype(BF16)
    return jnp.concatenate([hi, hi, lo], axis=1)


def kernel(ngx, ngy, src_h, kap_h, diag_h, faces_h, smooth_h, prol_h, both_out,
           held, s_out, src, kap, diag, faces, smooth, prol, s_in, q0, u1, u2, u3, q1, u11, u21, e1, q2, u12, u22, e2, pp, pb, rr,
           wm, wl, wb, wr, wp,
           s_q0, r_q0, s_qx, r_qx, s_qc, r_qc, s_u2b, r_u2b, s_g, r_g, s_rl, r_rl, s_q2, r_q2, s_u21, r_u21):
    sol, res = held.at[0], held.at[1]

    def store(i):
        return pltpu.make_async_copy(held.at[i], both_out.at[pl.ds(N * 8 * i, N * 8)], s_out.at[i])

    gx, gy = lax.axis_index("gx"), lax.axis_index("gy")

    def inside(dx, dy):
        ok = None
        for at, d, n in ((gx, dx, ngx), (gy, dy, ngy)):
            if d:
                c = (at + d >= 0) & (at + d < n)
                ok = c if ok is None else ok & c
        return ok

    fetches = [pltpu.make_async_copy(a, b, s_in.at[i]) for i, (a, b) in enumerate((
        (src_h, src), (kap_h, kap), (smooth_h, smooth), (faces_h, faces), (diag_h, diag), (prol_h, prol)))]
    for f in fetches:
        f.start()

    barrier = pltpu.get_barrier_semaphore()
    partners = [(d, 0) for d in (-3, -2, -1, 1, 2, 3)] + [(0, d) for d in (-3, -2, -1, 1, 2, 3)]
    partners += [(a, b) for a in (-1, 1) for b in (-1, 1)]
    for dx, dy in partners:
        @pl.when(inside(dx, dy))
        def _():
            pl.semaphore_signal(barrier, inc=1, device_id=(gx + dx, gy + dy), device_id_type=MESH)
    fetches[1].wait()
    fetches[0].wait()
    for y in range(2):
        for x in range(4):
            c = x * 2 + y
            q0[2 + y, 2 + x] = src[pl.ds(c, N, stride=8), :] / kap[pl.ds(c, 1), :]
    peers = 0
    for dx, dy in partners:
        peers = peers + inside(dx, dy).astype(jnp.int32)
    pl.semaphore_wait(barrier, peers)

    def remote(s, d, ssem, rsem, dx, dy):
        return pltpu.make_async_remote_copy(
            src_ref=s, dst_ref=d, send_sem=ssem, recv_sem=rsem,
            device_id=(gx + dx, gy + dy), device_id_type=MESH)

    def send(s, d, ssem, rsem, dx, dy, cond=None):
        ok = inside(dx, dy) if cond is None else cond

        @pl.when(ok)
        def _():
            remote(s, d, ssem, rsem, dx, dy).start()

    def receive(d, ssem, rsem, dx, dy, cond=None):
        ok = inside(dx, dy) if cond is None else cond

        @pl.when(ok)
        def _():
            remote(d, d, ssem, rsem, dx, dy).wait_recv()

    def clear(ref, dx, dy):
        @pl.when(jnp.logical_not(inside(dx, dy)))
        def _():
            ref[...] = jnp.zeros(ref.shape, F32)

    def faces_x(buf):
        return [
            (buf.at[pl.ds(2, 2), 5], buf.at[pl.ds(2, 2), 1], 1, 0),
            (buf.at[pl.ds(2, 2), 2], buf.at[pl.ds(2, 2), 6], -1, 0),
            (buf.at[pl.ds(2, 2), 4], buf.at[pl.ds(2, 2), 0], 1, 0),
            (buf.at[pl.ds(2, 2), 3], buf.at[pl.ds(2, 2), 7], -1, 0),
        ]

    def near_y(buf, x, n):
        return [
            (buf.at[3, pl.ds(x, n)], buf.at[1, pl.ds(x, n)], 0, 1),
            (buf.at[2, pl.ds(x, n)], buf.at[4, pl.ds(x, n)], 0, -1),
        ]

    def far_y(buf, x, n):
        return [
            (buf.at[2, pl.ds(x, n)], buf.at[0, pl.ds(x, n)], 0, 1),
            (buf.at[3, pl.ds(x, n)], buf.at[5, pl.ds(x, n)], 0, -1),
        ]

    def corners(buf):
        return [
            (buf.at[3, 5], buf.at[1, 1], 1, 1),
            (buf.at[3, 2], buf.at[1, 6], -1, 1),
            (buf.at[2, 5], buf.at[4, 1], 1, -1),
            (buf.at[2, 2], buf.at[4, 6], -1, -1),
        ]

    def send_all(faces_of, ssem, rsem):
        for i, (s, d, dx, dy) in enumerate(faces_of):
            send(s, d, ssem.at[i], rsem.at[i], dx, dy)

    def receive_all(faces_of, ssem, rsem):
        for i, (s, d, dx, dy) in enumerate(faces_of):
            receive(d, ssem.at[i], rsem.at[i], -dx, -dy)

    q0_y = near_y(q0, 2, 1) + near_y(q0, 5, 1) + near_y(q0, 3, 2) + far_y(q0, 2, 2) + far_y(q0, 4, 2)
    q0_x = faces_x(q0)
    q0_c = [
        (q0.at[1, 5], q0.at[1, 1], 1, -1),
        (q0.at[4, 5], q0.at[4, 1], 1, 1),
        (q0.at[1, 2], q0.at[1, 6], -1, -1),
        (q0.at[4, 2], q0.at[4, 6], -1, 1),
    ]
    u2_more = far_y(u2, 2, 4) + faces_x(u2)[2:] + corners(u2)
    send_all(q0_y, s_q0, r_q0)
    send_all(q0_x, s_qx, r_qx)

    for f in fetches[2:]:
        f.wait()
    s8 = OMEGA * smooth[...]
    eye = (lax.broadcasted_iota(jnp.int32, (N, N), 0) == lax.broadcasted_iota(jnp.int32, (N, N), 1)).astype(F32)
    wm[pl.ds(SM, N), :] = widen(s8)
    for i, at in enumerate(FACES):
        f = faces[i]
        wb[pl.ds(at, N), :] = widen(-f)
        sf = exact_dot(s8, f)
        wl[pl.ds(at, N), :] = widen(sf)
        wm[pl.ds(at, N), :] = widen(exact_dot(sf, s8))
    d = diag[...]
    wb[pl.ds(CC, N), :] = widen(d)
    lc = eye - exact_dot(s8, d)
    wl[pl.ds(CC, N), :] = widen(lc)
    wm[pl.ds(CC, N), :] = widen(s8 + exact_dot(lc, s8))
    for i in range(4):
        p = prol[i]
        wp[pl.ds(N * i, N), :] = widen(p)
        wr[pl.ds(N * i, N), :] = widen(0.25 * p.T)

    for group in (q0_y, q0_x, u2_more):
        for _, dst, dx, dy in group:
            clear(dst, -dx, -dy)
    for _, dst, dx, dy in q0_c:
        clear(dst, -dx, dy)
    clear(q1.at[pl.ds(0, 2)], -1, 0)
    clear(q1.at[pl.ds(4, 2)], 1, 0)
    clear(u21.at[0], -1, 0)
    clear(u21.at[5], 1, 0)
    for dd in (1, 2, 3):
        clear(q2.at[3 - dd], -dd, 0)
        clear(q2.at[3 + dd], dd, 0)
    e1[:, 0] = jnp.zeros((4, N, LANES), F32)
    e1[:, 5] = jnp.zeros((4, N, LANES), F32)

    lane = lax.broadcasted_iota(jnp.int32, (N, LANES), 1)
    not_first, not_last = lane > 0, lane < LANES - 1

    def apply(w, row, rows, load, cols, at, to=pp):
        pair = jnp.concatenate([split(load(cols[0])), split(load(cols[1]))], axis=1)
        out = jnp.dot(w[pl.ds(row, rows), :], pair, preferred_element_type=F32)
        to[at[0], pl.ds(row, rows), :] = out[:, :LANES]
        to[at[1], pl.ds(row, rows), :] = out[:, LANES:]

    def gathered(c, sx, sy, ym=True, yp=True, of=pp):
        t = of[c, pl.ds(CC, N), :]
        t = t + of[c - sx, pl.ds(XM, N), :] + of[c + sx, pl.ds(XP, N), :]
        if ym:
            t = t + of[c - sy, pl.ds(YM, N), :]
        if yp:
            t = t + of[c + sy, pl.ds(YP, N), :]
        t = t + jnp.where(not_first, pltpu.roll(of[c, pl.ds(ZM, N), :], 1, 1), 0.0)
        t = t + jnp.where(not_last, pltpu.roll(of[c, pl.ds(ZP, N), :], LANES - 1, 1), 0.0)
        return t

    def loop(n, body):
        for i in range(n):
            body(i)

    def fine_at(y, x):
        return (y + 2) * 8 + x + 2

    def fine(w, row, rows, buf, c, e, to=pp):
        apply(w, row, rows, lambda p: buf[2 + p[0], 2 + p[1]], (c, e), (fine_at(*c), fine_at(*e)), to)

    def fine_own(w, rows, buf, to=pp):
        for y in range(2):
            for x in (0, 2):
                fine(w, 0, rows, buf, (y, x), (y, x + 1), to)

    def keep(ok):
        return jnp.where(ok, 1.0, 0.0).astype(F32)

    def present(offset):
        return keep((gx + offset >= 0) & (gx + offset < ngx))

    def side(offset):
        return keep((gy + offset >= 0) & (gy + offset < ngy))

    def take_u2(y, x, m=None):
        c = fine_at(y, x)
        v = gathered(c, 1, 8)
        u2[2 + y, 2 + x] = v if m is None else m * v
        u1[1 + y, 1 + x] = pp[c, pl.ds(SM, N), :]

    fine_own(wm, 512, q0)
    receive_all(q0_x, s_qx, r_qx)
    for y in range(2):
        fine(wm, 0, 512, q0, (y, -1), (y, 4))
        fine(wm, XM, 128, q0, (y, -2), (y, 5))

    def forward(group):
        for i, (s, d, dx, dy) in group:
            @pl.when(inside(dx, 0) & inside(0, dy))
            def _():
                pltpu.make_async_remote_copy(
                    src_ref=s, dst_ref=d, send_sem=s_qc.at[i], recv_sem=r_qc.at[i],
                    device_id=(gx + dx, gy), device_id_type=MESH).start()

    def receive_part(first, n):
        for i in range(first, first + n):
            s, d, dx, dy = q0_y[i]
            receive(d, s_q0.at[i], r_q0.at[i], -dx, -dy)

    receive_part(2, 2)
    forward([(0, q0_c[0]), (1, q0_c[1])])
    receive_part(0, 2)
    forward([(2, q0_c[2]), (3, q0_c[3])])
    receive_part(4, 2)
    for x in range(4):
        fine(wm, 0, 512, q0, (-1, x), (2, x))
    for y in range(2):
        for x in range(4):
            take_u2(y, x)
    fine_own(wb, 448, u2, pb)
    for i, (s, d, dx, dy) in enumerate(q0_c):
        @pl.when(inside(-dx, 0) & inside(0, dy))
        def _():
            pltpu.make_async_remote_copy(
                src_ref=d, dst_ref=d, send_sem=s_qc.at[i], recv_sem=r_qc.at[i],
                device_id=(gx - dx, gy), device_id_type=MESH).wait_recv()
    for y in (-1, 2):
        fine(wm, 0, 256, q0, (y, -1), (y, 4))
    for y in range(2):
        take_u2(y, -1, present(-1))
        take_u2(y, 4, present(1))
        fine(wb, XM, 128, u2, (y, -1), (y, 4), pb)

    def relay(j, at):
        for i, (dx, to) in enumerate(((1, 0), (-1, 4))):
            @pl.when(inside(dx, 0))
            def _():
                remote(q1.at[2 + at, j, pl.ds(0, N)], q1.at[to + at, j, pl.ds(0, N)], s_rl.at[i, at, j], r_rl.at[i, at, j], dx, 0).start()

    def half(at):
        receive_part(6 + 2 * at, 2)
        for x in (2 * at, 2 * at + 1):
            fine(wm, YM, 128, q0, (-2, x), (3, x))
        for x in (2 * at, 2 * at + 1):
            take_u2(-1, x, side(-1))
            take_u2(2, x, side(1))
        for x in (2 * at, 2 * at + 1):
            fine(wb, YM, 128, u2, (-1, x), (2, x), pb)
        total = None
        for x in (2 * at, 2 * at + 1):
            for y in range(2):
                t = gathered(fine_at(y, x), 1, 8, of=pb)
                k = kap[pl.ds(x * 2 + y, 1), :]
                r = split((q0[2 + y, 2 + x] - t) * k)
                child = 2 * (x - 2 * at) + y
                part = jnp.dot(wr[pl.ds(N * child, N), :], r, preferred_element_type=F32)
                total = part if total is None else total + part
        k1 = kap[pl.ds(4 * at, 1), :] + kap[pl.ds(4 * at + 1, 1), :]
        k1 = (k1 + (kap[pl.ds(4 * at + 2, 1), :] + kap[pl.ds(4 * at + 3, 1), :])) * 0.25
        q1[2 + at, gy, pl.ds(0, N), :] = total / k1
        q1[2 + at, gy, pl.ds(N, 8), :] = jnp.broadcast_to(k1, (8, LANES))
        for j in range(ngy):
            @pl.when(gy != j)
            def _():
                pltpu.make_async_remote_copy(
                    src_ref=q1.at[2 + at, gy], dst_ref=q1.at[2 + at, gy],
                    send_sem=s_g.at[at, j], recv_sem=r_g.at[at, gy],
                    device_id=(gx, j), device_id_type=MESH).start()
        relay(gy, at)

    half(0)
    half(1)

    def restrict(index):
        total = None
        for child in range(4):
            pair = jnp.concatenate([rr[index(0, child)], rr[index(1, child)]], axis=1)
            part = jnp.dot(wr[pl.ds(N * child, N), :], pair, preferred_element_type=F32)
            total = part if total is None else total + part
        return total[:, :LANES], total[:, LANES:]

    def arrive(j, at):
        block = q1.at[2 + at, j]
        pltpu.make_async_remote_copy(
            src_ref=block, dst_ref=block, send_sem=s_g.at[at, j], recv_sem=r_g.at[at, j],
            device_id=(gx, j), device_id_type=MESH).wait_recv()
        relay(j, at)
    for at in range(2):
        for dd in (1, -1, 2, -2, 3, -3):
            @pl.when(inside(0, dd))
            def _():
                arrive(gy + dd, at)
    send_all(u2_more, s_u2b, r_u2b)

    def coarse_own(w, rows, load, first, planes):
        def body(i):
            c = 4 * first + 2 * i
            apply(w, 0, rows, load, (c, c + 1), (c, c + 1))
        loop(2 * planes, body)

    def coarse_edges(w, load, low, high):
        def body(y):
            c, e = 4 * low + y, 4 * high + y
            apply(w, XM, 128, load, (c, e), (c, e))
        loop(4, body)

    def load_q1(c):
        return q1[c // 4, c % 4, pl.ds(0, N), :]

    def load_u21(c):
        return u21[c // 4, c % 4]

    coarse_own(wm, 512, load_q1, 2, 2)
    for at in range(2):
        for j in range(ngy):
            for i, (dx, to) in enumerate(((1, 0), (-1, 4))):
                @pl.when(inside(-dx, 0))
                def _():
                    block = q1.at[to + at, j, pl.ds(0, N)]
                    remote(block, block, s_rl.at[i, at, j], r_rl.at[i, at, j], -dx, 0).wait_recv()
        coarse_own(wm, 512, load_q1, 1 if at else 4, 1)
    coarse_edges(wm, load_q1, 0, 5)

    def device_of(x):
        return (x // 2) - 1

    def sum_u21(x):
        m = present(device_of(x))
        for y in range(4):
            c = 4 * x + y
            u21[x, y] = m * gathered(c, 4, 1, y > 0, y < 3)
            u11[x, y] = m * pp[c, pl.ds(SM, N), :]
    loop(4, lambda i: sum_u21(i + 1))

    low = pl.ds(jnp.clip(gy - 1, 0, ngy - 3), 3)
    u21_moves = [(u21.at[2, low], u21.at[0, low], 1, 0), (u21.at[3, low], u21.at[5, low], -1, 0)]
    coarse_own(wb, 448, load_u21, 2, 2)
    coarse_edges(wb, load_u21, 1, 4)

    def sum_r1(x):
        for y in range(4):
            t = gathered(4 * x + y, 4, 1, y > 0, y < 3)
            k1 = q1[x, y, pl.ds(N, 1), :]
            rr[(x - 2) * 4 + y] = split((q1[x, y, pl.ds(0, N), :] - t) * k1)
    loop(2, lambda i: sum_r1(i + 2))
    coarse2 = restrict(lambda at, child: (child // 2) * 4 + 2 * at + child % 2)
    for at in range(2):
        k2 = q1[2, 2 * at, pl.ds(N, 1), :] + q1[2, 2 * at + 1, pl.ds(N, 1), :]
        k2 = (k2 + (q1[3, 2 * at, pl.ds(N, 1), :] + q1[3, 2 * at + 1, pl.ds(N, 1), :])) * 0.25
        q2[3, at] = coarse2[at] / k2

    q2_moves = [(q2.at[3], q2.at[3 - dd], dd, 0) for dd in (1, -1, 2, -2, 3, -3)]
    send_all(q2_moves, s_q2, r_q2)
    send_all(u21_moves, s_u21, r_u21)

    def load_q2(c):
        return q2[c // 2, c % 2]

    def load_u22(c):
        return u22[c // 2, c % 2]

    def last_own(w, rows, load, first, planes):
        def body(i):
            c = 2 * first + 2 * i
            apply(w, 0, rows, load, (c, c + 1), (c, c + 1))
        loop(planes, body)

    def last_edges(w, load, low, high):
        def body(y):
            c, e = 2 * low + y, 2 * high + y
            apply(w, XM, 128, load, (c, e), (c, e))
        loop(2, body)

    last_own(wm, 512, load_q2, 3, 1)
    for group, ssem, rsem in ((q0_y, s_q0, r_q0), (q0_x, s_qx, r_qx)):
        for i, (s, dst, dx, dy) in enumerate(group):
            @pl.when(inside(dx, dy))
            def _():
                remote(s, dst, ssem.at[i], rsem.at[i], dx, dy).wait_send()
    for i, (s, d, dx, dy) in enumerate(q0_c):
        @pl.when(inside(dx, 0) & inside(0, dy))
        def _():
            pltpu.make_async_remote_copy(
                src_ref=s, dst_ref=d, send_sem=s_qc.at[i], recv_sem=r_qc.at[i],
                device_id=(gx + dx, gy), device_id_type=MESH).wait_send()
    for at in range(2):
        for j in range(ngy):
            block = q1.at[2 + at, j]

            @pl.when(gy != j)
            def _():
                pltpu.make_async_remote_copy(
                    src_ref=block, dst_ref=block, send_sem=s_g.at[at, j], recv_sem=r_g.at[at, j],
                    device_id=(gx, j), device_id_type=MESH).wait_send()
            for i, (dx, to) in enumerate(((1, 0), (-1, 4))):
                @pl.when(inside(dx, 0))
                def _():
                    remote(block.at[pl.ds(0, N)], q1.at[to + at, j, pl.ds(0, N)], s_rl.at[i, at, j], r_rl.at[i, at, j], dx, 0).wait_send()
    def receive_q2(distance):
        for i, (s, d, dx, dy) in enumerate(q2_moves):
            if abs(dx) == distance:
                receive(d, s_q2.at[i], r_q2.at[i], -dx, -dy)

    receive_q2(1)
    last_own(wm, 512, load_q2, 2, 1)
    last_own(wm, 512, load_q2, 4, 1)
    receive_q2(2)
    last_own(wm, 512, load_q2, 1, 1)
    last_own(wm, 512, load_q2, 5, 1)
    receive_q2(3)
    last_edges(wm, load_q2, 0, 6)

    def sum_u22(x):
        m = present(x - 3)
        for y in range(2):
            u22[x, y] = m * gathered(2 * x + y, 2, 1, y > 0, y < 1)
            u12[x, y] = pp[2 * x + y, pl.ds(SM, N), :]
    loop(5, lambda i: sum_u22(i + 1))
    last_own(wl, 448, load_u22, 2, 3)
    last_edges(wl, load_u22, 1, 5)

    def sum_e2(x):
        m = present(x - 3)
        for y in range(2):
            e2[x - 2, y] = m * (u12[x, y] + gathered(2 * x + y, 2, 1, y > 0, y < 1))
    loop(3, lambda i: sum_e2(i + 2))

    receive_all(u21_moves, s_u21, r_u21)

    def prolong(load):
        pair = jnp.concatenate([split(load(0)), split(load(1))], axis=1)
        out = jnp.dot(wp[...], pair, preferred_element_type=F32)
        return lambda at, child: out[N * child:N * (child + 1), LANES * at:LANES * (at + 1)]

    for i, (s, dst, dx, dy) in enumerate(q2_moves):
        @pl.when(inside(dx, dy))
        def _():
            remote(s, dst, s_q2.at[i], r_q2.at[i], dx, dy).wait_send()

    for i, (s, dst, dx, dy) in enumerate(u21_moves):
        @pl.when(inside(dx, dy))
        def _():
            remote(s, dst, s_u21.at[i], r_u21.at[i], dx, dy).wait_send()

    def lift1(x2):
        part = prolong(lambda y: e2[x2, y])
        for y2 in range(2):
            for child in range(4):
                x, y = 2 * x2 + child // 2, 2 * y2 + child % 2
                u21[x, y] = u21[x, y] + part(y2, child)
    loop(3, lift1)
    coarse_own(wl, 448, load_u21, 1, 4)
    coarse_edges(wl, load_u21, 0, 5)

    def sum_e1(x):
        m = present(device_of(x))
        for y in range(4):
            e1[x - 1, 1 + y] = m * (u11[x, y] + gathered(4 * x + y, 4, 1, y > 0, y < 3))
    loop(4, lambda i: sum_e1(i + 1))

    receive_all(u2_more, s_u2b, r_u2b)
    for i, (s, dst, dx, dy) in enumerate(u2_more):
        @pl.when(inside(dx, dy))
        def _():
            remote(s, dst, s_u2b.at[i], r_u2b.at[i], dx, dy).wait_send()

    wanted = {(y, x) for y in range(-2, 4) for x in range(-2, 6)
              if max(0, -y, y - 1) + max(0, -x, x - 3) <= 2}
    for j in range(3):
        for xp in range(2):
            part = prolong(lambda i: e1[2 * xp + i, gy + j])
            for i in range(2):
                for child in range(4):
                    x = 2 * (2 * xp + i - 1) + child // 2
                    y = 2 * (j - 1) + child % 2
                    if (y, x) in wanted:
                        u2[2 + y, 2 + x] = u2[2 + y, 2 + x] + part(i, child)

    def load_u2(c):
        return u2[2 + c[0], 2 + c[1]]

    def both(w, row, rows, c, e):
        apply(w, row, rows, load_u2, (c, e), (fine_at(*c), fine_at(*e)))

    def rows_wide(i):
        y, x = i // 3, (i % 3) * 2 - 1
        both(wl, 0, 448, (y, x), (y, x + 1))
    loop(6, rows_wide)

    def rows_short(i):
        y, x = (i // 2) * 3 - 1, (i % 2) * 2
        both(wl, 0, 448, (y, x), (y, x + 1))
    loop(4, rows_short)
    loop(2, lambda y: both(wl, XM, 128, (y, -2), (y, 5)))
    loop(4, lambda x: both(wl, YM, 128, (-2, x), (3, x)))
    loop(2, lambda i: both(wl, 0, 256, (3 * i - 1, -1), (3 * i - 1, 4)))

    def sum_u3(y, x, m=None):
        v = u1[1 + y, 1 + x] + gathered(fine_at(y, x), 1, 8)
        u3[2 + y, 2 + x] = v if m is None else m * v
        return v

    def own_u3(i):
        y, x = i // 4, i % 4
        v = sum_u3(y, x)
        sol[pl.ds(x * 2 + y, N, stride=8), :] = v
    loop(8, own_u3)
    store(0).start()
    loop(2, lambda y: sum_u3(y, -1, present(-1)))
    loop(2, lambda y: sum_u3(y, 4, present(1)))
    loop(4, lambda x: sum_u3(-1, x, keep(gy > 0)))
    loop(4, lambda x: sum_u3(2, x, keep(gy < ngy - 1)))
    fine_own(wb, 448, u3)
    for y in range(2):
        fine(wb, XM, 128, u3, (y, -1), (y, 4))
    for x in range(4):
        fine(wb, YM, 128, u3, (-1, x), (2, x))

    def final(i):
        y, x = i // 4, i % 4
        c = x * 2 + y
        t = gathered(fine_at(y, x), 1, 8)
        res[pl.ds(c, N, stride=8), :] = src[pl.ds(c, N, stride=8), :] - kap[pl.ds(c, 1), :] * t
    loop(8, final)
    store(1).start()

    store(0).wait()
    store(1).wait()


def solution(mesh):
    ngx, ngy = mesh.shape["gx"], mesh.shape["gy"]

    def shards(source, conductivity, diag_block, face_blocks, smoother, prolong):
        dma = pltpu.SemaphoreType.DMA
        col = (N, LANES)
        scratch = [
            pltpu.VMEM((2, N * 8, LANES), F32),
            dma((2,)),
            pltpu.VMEM((N * 8, LANES), F32),
            pltpu.VMEM((8, LANES), F32),
            pltpu.VMEM((N, N), F32),
            pltpu.VMEM((6, N, N), F32),
            pltpu.VMEM((N, N), F32),
            pltpu.VMEM((4, N, N), F32),
            dma((6,)),
            pltpu.VMEM((6, 8) + col, F32),
            pltpu.VMEM((4, 6) + col, F32),
            pltpu.VMEM((6, 8) + col, F32),
            pltpu.VMEM((6, 8) + col, F32),
            pltpu.VMEM((6, 4, N + 8, LANES), F32),
            pltpu.VMEM((6, 4) + col, F32),
            pltpu.VMEM((6, 4) + col, F32),
            pltpu.VMEM((4, 6) + col, F32),
            pltpu.VMEM((7, 2) + col, F32),
            pltpu.VMEM((7, 2) + col, F32),
            pltpu.VMEM((7, 2) + col, F32),
            pltpu.VMEM((3, 2) + col, F32),
            pltpu.VMEM((48, 512, LANES), F32),
            pltpu.VMEM((48, 448, LANES), F32),
            pltpu.VMEM((8, 192, LANES), BF16),
            pltpu.VMEM((512, 192), BF16),
            pltpu.VMEM((448, 192), BF16),
            pltpu.VMEM((448, 192), BF16),
            pltpu.VMEM((256, 192), BF16),
            pltpu.VMEM((256, 192), BF16),
            dma((10,)), dma((10,)), dma((4,)), dma((4,)), dma((4,)), dma((4,)), dma((8,)), dma((8,)),
            dma((2, 4)), dma((2, 4)), dma((2, 2, 4)), dma((2, 2, 4)), dma((6,)), dma((6,)), dma((2,)), dma((2,)),
        ]
        shape = source.shape
        flat = jax.ShapeDtypeStruct((2 * N * 8, LANES), F32)
        both = pl.pallas_call(
            functools.partial(kernel, ngx, ngy),
            out_shape=flat,
            in_specs=[pl.BlockSpec(memory_space=pl.ANY)] * 6,
            out_specs=pl.BlockSpec(memory_space=pl.ANY),
            scratch_shapes=scratch,
            compiler_params=pltpu.CompilerParams(
                collective_id=0, has_side_effects=True, vmem_limit_bytes=60 << 20),
            cost_estimate=pl.CostEstimate(flops=10**9, bytes_accessed=10**6, transcendentals=0),
        )(source.reshape(N * 8, LANES), conductivity.reshape(8, LANES),
          diag_block, face_blocks, smoother, prolong)
        return both[:N * 8].reshape(shape), both[N * 8:].reshape(shape)

    return jax.shard_map(
        shards,
        mesh=mesh,
        in_specs=(P(None, "gx", "gy", None), P("gx", "gy", None), P(), P(), P(), P()),
        out_specs=(P(None, "gx", "gy", None), P(None, "gx", "gy", None)),
        check_vma=False,
    )
```
